128 devices in a mesh: section: 2 (over core), dp: 64 (over y, x, z).
Axes of the slice: x: 4, y: 4, z: 4, core: 2. Of those that a mesh axis runs over, the one named last changes fastest.
Arguments:
- tokens: bfloat16 [128, 64, 768], P('dp', 'section'), may hold values from -6 to 6
- out_grad: bfloat16 [128, 64, 768], P('dp', 'section'), may hold values from -6 to 6
- passes: int32 [128], P('dp'), may hold values from 2 to 5
- pass_embed: float32 [5, 768], replicated, may hold values from -3 to 3
- qkv_weight: bfloat16 [2, 768, 2304], P('section'), may hold values from -0.21875 to 0.21875
- out_weight: bfloat16 [2, 768, 768], P('section'), may hold values from -0.875 to 0.875
- up_weight: bfloat16 [2, 768, 3072], P('section'), may hold values from -0.21875 to 0.21875
- down_weight: bfloat16 [2, 3072, 768], P('section'), may hold values from -0.109375 to 0.109375
- norm_gains: float32 [2, 2, 768], P('section'), may hold values from 0.1 to 1.9
- bias_rows: float32 [2, 6, 768], P('section'), may hold values from -1.8 to 1.8
- up_bias: float32 [2, 3072], P('section'), may hold values from -1.8 to 1.8
Outputs:
- hidden_out: bfloat16 [128, 64, 768], P('dp', 'section')
- token_grad: bfloat16 [128, 64, 768], P('dp', 'section')
- grad_qkv_weight: float32 [2, 768, 2304], P('section', 'dp')
- grad_out_weight: float32 [2, 768, 768], P('section', 'dp')
- grad_up_weight: float32 [2, 768, 3072], P('section', 'dp')
- grad_down_weight: float32 [2, 3072, 768], P('section', 'dp')
- grad_norm_gains: float32 [2, 2, 768], P('section', None, 'dp')
- grad_bias_rows: float32 [2, 6, 768], P('section', None, 'dp')
- grad_up_bias: float32 [2, 3072], P('section', 'dp')
- grad_pass_embed: float32 [5, 768], P(None, ('section', 'dp'))
The draws below stay inside these ranges and needn't reach their ends.
All inputs are finite; a program needn't handle non-finite values.
Results may differ from the reference program's by a relative error of at most 0.017.
Values may be sent and summed in bfloat16 or wider, within the bound.
A program may use at most 256 MiB of HBM per device.

```python
import math
import jax
import jax.numpy as jnp
from jax import lax

D = 768
HEADS = 12
HEAD_DIM = 64
FF = 3072
BASE = 64
MAXP = 5
SEQS = 128


def place_ends(values, stream_key, smallest, largest):
    place = [jax.random.randint(jax.random.fold_in(stream_key, axis), (), 0, length) for axis, length in enumerate(values.shape)]
    main_axis = values.shape.index(max(values.shape))
    next_to = place[:main_axis] + [(place[main_axis] + 1) % values.shape[main_axis]] + place[main_axis + 1:]
    return values.at[tuple(place)].set(smallest).at[tuple(next_to)].set(largest)


def block_scale(rng, shape, cuts, least, high):
    level, own = 1.0, jax.random.fold_in(rng, 6)
    for position, shards_of in cuts:
        heights = jnp.exp(jax.random.uniform(jax.random.fold_in(own, position), (shards_of,), jnp.float32, least / len(cuts), high / len(cuts)))
        level = level * jnp.repeat(heights, shape[position] // shards_of).reshape([-1 if axis == position else 1 for axis in range(len(shape))])
    return level


def normal_values(key, extent, scale, limit, split=(), dtype=jnp.bfloat16):
    values = scale * jax.random.normal(key, extent, jnp.float32)
    if split:
        values = values * block_scale(key, extent, split, -0.22, 0.18)
    return jnp.clip(values, -limit, limit).astype(dtype)


def setup_inputs(seed: int = 0) -> dict:
    seeds = jax.random.split(jax.random.key(seed), 12)
    return {
        "tokens": normal_values(seeds[0], (SEQS, BASE, D), 1.0, 6.0, ((0, 64), (1, 2))),
        "out_grad": normal_values(seeds[1], (SEQS, BASE, D), 1.0, 6.0, ((0, 64), (1, 2))),
        "passes": place_ends(jax.random.randint(seeds[2], (SEQS,), 2, MAXP + 1), jax.random.fold_in(seeds[2], 1), 2, MAXP).astype(jnp.int32),
        "pass_embed": normal_values(seeds[3], (MAXP, D), 0.5, 3.0, (), jnp.float32),
        "qkv_weight": normal_values(seeds[4], (2, D, 3 * D), D ** -0.5, 0.21875, ((0, 2),)),
        "out_weight": normal_values(seeds[5], (2, D, D), (D // 16) ** -0.5, 0.875, ((0, 2),)),
        "up_weight": normal_values(seeds[6], (2, D, FF), D ** -0.5, 0.21875, ((0, 2),)),
        "down_weight": normal_values(seeds[7], (2, FF, D), FF ** -0.5, 0.109375, ((0, 2),)),
        "norm_gains": jnp.clip(1.0 + 0.18 * jax.random.normal(seeds[8], (2, 2, D), jnp.float32), 0.1, 1.9),
        "bias_rows": normal_values(seeds[9], (2, 6, D), 0.3, 1.8, ((0, 2),), jnp.float32),
        "up_bias": normal_values(seeds[10], (2, FF), 0.3, 1.8, ((0, 2),), jnp.float32),
    }


@jax.custom_vjp
def low(v):
    return lax.optimization_barrier(v.astype(jnp.bfloat16)).astype(jnp.float32)

@jax.custom_vjp
def low_back(v):
    return v

def low_keep(v):
    return (low(v), None)

def low_pass(kept, grad):
    return (grad,)

def back_keep(v):
    return (v, None)

def back_low(kept, grad):
    return (low(grad),)
low.defvjp(low_keep, low_pass)
low_back.defvjp(back_keep, back_low)
HIGHEST = lax.Precision.HIGHEST

def layer_norm(values, gain, shift):
    centre = values - lax.optimization_barrier(jnp.mean(values, -1, keepdims=True))
    spread = lax.optimization_barrier(jnp.mean(centre * centre, -1, keepdims=True))
    return centre * lax.rsqrt(spread + 1e-05) * gain + shift

def gelu_tanh(values):
    return jax.nn.gelu(values, approximate=True)

def allowed_keys(query_count, key_count, slot_index):
    key_pos = lax.broadcasted_iota(jnp.int32, (1, 1, key_count), 2)
    query_pos = lax.broadcasted_iota(jnp.int32, (1, query_count, 1), 1)
    return (key_pos // query_count <= slot_index) & (key_pos % query_count <= query_pos)

def attend(query, key_rows, value_rows, slot_index):
    row_count = query.shape[0]
    heads_q = query.reshape(row_count, HEADS, HEAD_DIM)
    heads_k = key_rows.reshape(-1, HEADS, HEAD_DIM)
    heads_v = value_rows.reshape(-1, HEADS, HEAD_DIM)
    scores = jnp.einsum('qhd,khd->hqk', heads_q, heads_k, precision=HIGHEST) * (1.0 / math.sqrt(HEAD_DIM))
    scores = low_back(scores)
    scores = jnp.where(allowed_keys(row_count, heads_k.shape[0], slot_index), scores, -1e+30)
    weights = jnp.exp(scores - lax.optimization_barrier(jnp.max(scores, -1, keepdims=True)))
    attention = low(weights / lax.optimization_barrier(jnp.sum(weights, -1, keepdims=True)))
    mixed = jnp.einsum('hqk,khd->qhd', attention, heads_v, precision=HIGHEST)
    return mixed.reshape(row_count, HEADS * HEAD_DIM)

def apply_block(slot_input, layer, slot_index, key_rows, value_rows):
    qkv_weight, out_weight, up_weight, down_weight, gain_rows, bias_rows, up_bias = layer
    row_count, width = slot_input.shape
    normed = low(layer_norm(slot_input, gain_rows[0], bias_rows[0]))
    qkv_bias = jnp.concatenate([bias_rows[1], jnp.zeros_like(bias_rows[1]), bias_rows[2]])
    projected = low_back(low(jnp.dot(normed, qkv_weight, precision=HIGHEST) + qkv_bias))
    query = projected[:, :width]
    lower = slot_index * row_count
    key_rows = key_rows.at[lower:lower + row_count].set(projected[:, width:2 * width])
    value_rows = value_rows.at[lower:lower + row_count].set(projected[:, 2 * width:])
    mixed = low_back(low(attend(query, key_rows, value_rows, slot_index)))
    branch = low_back(jnp.dot(mixed, out_weight, precision=HIGHEST) + bias_rows[3])
    middle = slot_input + branch
    normed_two = low(layer_norm(middle, gain_rows[1], bias_rows[4]))
    hidden = low_back(jnp.dot(normed_two, up_weight, precision=HIGHEST) + up_bias)
    active = low(gelu_tanh(hidden))
    result = middle + low_back(jnp.dot(active, down_weight, precision=HIGHEST) + bias_rows[5])
    return (result, key_rows, value_rows)

def sequence(tokens_seq, pass_count, layers, pass_embed):
    first_layer = tuple((param[0] for param in layers))
    later_layer = tuple((param[1] for param in layers))
    row_count, width = tokens_seq.shape
    empty = jnp.zeros(((MAXP - 1) * row_count, width), jnp.float32)
    result, _, _ = apply_block(tokens_seq + pass_embed[0], first_layer, 0, empty, empty)
    state = low_back(low(result))
    key_rows, value_rows = (empty, empty)
    for slot_index in range(MAXP - 1):
        result, key_rows, value_rows = apply_block(state + pass_embed[slot_index + 1], later_layer, slot_index, key_rows, value_rows)
        state = jnp.where(slot_index + 1 < pass_count, result, state)
    return state

def reference(tokens, out_grad, passes, pass_embed, qkv_weight, out_weight, up_weight, down_weight, norm_gains, bias_rows, up_bias):
    inputs = tokens.astype(jnp.float32)
    layers = tuple((param.astype(jnp.float32) for param in (qkv_weight, out_weight, up_weight, down_weight, norm_gains, bias_rows, up_bias)))

    def forward(input_states, layer_params, embed_rows):

        def scan_step(scan_carry, scan_item):
            tokens_seq, pass_count = scan_item

            def per_sequence(seq_values, seq_layers, seq_embed):
                return sequence(seq_values, pass_count, seq_layers, seq_embed)
            return (scan_carry, jax.checkpoint(per_sequence)(tokens_seq, layer_params, embed_rows))
        _, outputs = lax.scan(scan_step, jnp.zeros((), jnp.float32), (input_states, passes))
        return outputs
    outputs, pull = jax.vjp(forward, inputs, layers, pass_embed)
    input_grad, layer_grads, embed_grad = pull(out_grad.astype(jnp.float32))
    return (outputs.astype(jnp.bfloat16), input_grad.astype(jnp.bfloat16), layer_grads[0], layer_grads[1], layer_grads[2], layer_grads[3], layer_grads[4], layer_grads[5], layer_grads[6], embed_grad)
```

```python
import jax
import jax.numpy as jnp
import numpy as np
from jax import lax
from jax.experimental import pallas as pl
from jax.experimental.pallas import tpu as pltpu
from jax.sharding import PartitionSpec as P

F32 = jnp.float32
BF16 = jnp.bfloat16
VM = pltpu.VMEM
MESH = pl.DeviceIdType.MESH
D = 768
FF = 3072
SEQ = 64
R = 2 * SEQ
SLOTS = 4
ROWS = SLOTS * R
STEP = 256
STRIDE = {"y": 16, "x": 4, "z": 1}


class Names:
    def __init__(self, **entries):
        self.__dict__.update(entries)


def nn(a, b):
    return jnp.dot(a, b, preferred_element_type=F32)


def nt(a, b):
    return lax.dot_general(a, b, (((1,), (1,)), ((), ())), preferred_element_type=F32)


def tn(a, b):
    return lax.dot_general(a, b, (((0,), (0,)), ((), ())), preferred_element_type=F32)


def lane_masks(value, dtype):
    lane = lax.broadcasted_iota(jnp.int32, (1, STEP), 1) // 64
    return [jnp.where(lane == h, value, 0.0).astype(dtype) for h in range(4)]


def norm_forward(u, gain, shift, hat_ref, inv_ref):
    out = []
    for r in range(0, R, 32):
        v = u[r:r + 32]
        centre = v - jnp.sum(v, -1, keepdims=True) * (1.0 / D)
        inv = lax.rsqrt(jnp.sum(centre * centre, -1, keepdims=True) * (1.0 / D) + 1e-5)
        hat = centre * inv
        hat_ref[r:r + 32] = hat
        inv_ref[r:r + 32] = jnp.broadcast_to(inv, (32, 128))
        out.append((hat * gain + shift).astype(BF16))
    return jnp.concatenate(out, 0)


def norm_backward(dy, gain, hat_ref, inv_ref):
    out, dgain, dshift = [], 0.0, 0.0
    for r in range(0, R, 32):
        g = dy[r:r + 32]
        hat = hat_ref[r:r + 32]
        inv = inv_ref[r:r + 32][:, :1]
        dgain = dgain + jnp.sum(g * hat, 0, keepdims=True)
        dshift = dshift + jnp.sum(g, 0, keepdims=True)
        gg = g * gain
        m1 = jnp.sum(gg, -1, keepdims=True) * (1.0 / D)
        m2 = jnp.sum(gg * hat, -1, keepdims=True) * (1.0 / D)
        out.append((gg - m1 - hat * m2) * inv)
    return jnp.concatenate(out, 0), dgain, dshift


def keys_of(j):
    return 128 if j < 2 else 256


def forward(j, u, w, p, s):
    rows = slice(j * R, (j + 1) * R)
    a = norm_forward(u, p.gain(0), p.bias(0), s.hat1.at[j], s.inv1.at[j])
    s.a[rows] = a
    w.wait(0)
    for n in range(0, 3 * D, STEP):
        c = nn(a, w.qkv[:, n:n + STEP])
        k = n % D
        if n < D:
            s.q[j, :, k:k + STEP] = (c + p.bias(1)[:, k:k + STEP]).astype(BF16)
        elif n < 2 * D:
            c = c.astype(BF16)
            for q in range(2):
                s.k[q, j * SEQ:(j + 1) * SEQ, k:k + STEP] = c[q * SEQ:(q + 1) * SEQ]
        else:
            c = (c + p.bias(2)[:, k:k + STEP]).astype(BF16)
            for q in range(2):
                s.v[q, j * SEQ:(j + 1) * SEQ, k:k + STEP] = c[q * SEQ:(q + 1) * SEQ]
    nk = keys_of(j)
    ones = lane_masks(1.0, F32)
    eighth = lane_masks(0.125, BF16)
    col = lax.broadcasted_iota(jnp.int32, (SEQ, nk), 1)
    row = lax.broadcasted_iota(jnp.int32, (SEQ, nk), 0)
    allow = ((col & 63) <= row) & (col < (j + 1) * SEQ)
    veto = jnp.where(allow, 0.0, -1e30)
    veto = jnp.concatenate([veto] * 4, 0)
    for q in range(2):
        qrows = slice(q * SEQ, (q + 1) * SEQ)
        for g in range(3):
            cols = slice(g * STEP, (g + 1) * STEP)
            q4 = s.q[j, qrows, cols]
            q4 = jnp.concatenate([q4 * m for m in eighth], 0)
            sc = nt(q4, s.k[q, 0:nk, cols]) + veto
            ex = jnp.exp(sc - jnp.max(sc, -1, keepdims=True))
            pr = ex * (1.0 / jnp.sum(ex, -1, keepdims=True))
            s.p[j, 3 * q + g, :, 0:nk] = pr
            o4 = nn(pr.astype(BF16), s.v[q, 0:nk, cols])
            o = sum(o4[h * SEQ:(h + 1) * SEQ] * ones[h] for h in range(4))
            s.o[j * R + q * SEQ:j * R + (q + 1) * SEQ, cols] = o.astype(BF16)
    o = s.o[rows]
    w.wait(1)
    m1 = u + (jnp.concatenate([nn(o, w.out[:, n:n + STEP]) for n in range(0, D, STEP)], 1) + p.bias(3))
    b = norm_forward(m1, p.gain(1), p.bias(4), s.hat2.at[j], s.inv2.at[j])
    s.b[rows] = b
    w.wait(2)
    for n in range(0, FF, STEP):
        f = nn(b, w.up[:, n:n + STEP]) + p.up(n, n + STEP)
        t = jnp.tanh(0.7978845608 * (f + 0.044715 * f * f * f))
        half = 0.5 * (1.0 + t)
        s.e[rows, n:n + STEP] = (f * half).astype(BF16)
        s.slope[j, :, n:n + STEP] = half + 0.5 * f * (1.0 - t * t) * (
            0.7978845608 + 0.7978845608 * 3 * 0.044715 * f * f)
    e = s.e[rows]
    w.wait(3)
    r = jnp.concatenate([nn(e, w.down[:, n:n + STEP]) for n in range(0, D, STEP)], 1)
    return m1 + (r + p.bias(5))


def backward(j, dr, w, p, s, t, last):
    rows = slice(j * R, (j + 1) * R)
    dr2 = dr.astype(BF16)
    s.dr[rows] = dr2
    for n in range(0, FF, STEP):
        de = nt(dr2, w.down[n:n + STEP, :])
        s.df[rows, n:n + STEP] = (s.slope[j, :, n:n + STEP] * de).astype(BF16)
    df = s.df[rows]
    db = jnp.concatenate([nt(df, w.up[n:n + STEP, :]) for n in range(0, D, STEP)], 1)
    dm, dgain, dshift = norm_backward(db, p.gain(1), s.hat2.at[j], s.inv2.at[j])
    t.add(1, dgain)
    t.add(2 + 4, dshift)
    dm1 = dr + dm
    dz = dm1.astype(BF16)
    s.dz[rows] = dz
    for n in range(0, D, STEP):
        s.do[:, n:n + STEP] = nt(dz, w.out[n:n + STEP, :]).astype(BF16)
    nk = keys_of(j)
    ones = lane_masks(1.0, BF16)
    eighth = lane_masks(0.125, BF16)
    eighth32 = lane_masks(0.125, F32)
    for q in range(2):
        qrows = slice(q * SEQ, (q + 1) * SEQ)
        drows = slice(j * R + q * SEQ, j * R + (q + 1) * SEQ)
        for g in range(3):
            cols = slice(g * STEP, (g + 1) * STEP)
            do4 = s.do[qrows, cols]
            do4 = jnp.concatenate([do4 * m for m in ones], 0)
            q4 = s.q[j, qrows, cols]
            q4 = jnp.concatenate([q4 * m for m in eighth], 0)
            dp = nt(do4, s.v[q, 0:nk, cols])
            pr = s.p[j, 3 * q + g, :, 0:nk]
            ds = (pr * (dp - jnp.sum(pr * dp, -1, keepdims=True))).astype(BF16)
            dq4 = nn(ds, s.k[q, 0:nk, cols])
            dq = sum(dq4[h * SEQ:(h + 1) * SEQ] * eighth32[h] for h in range(4))
            s.dc[drows, cols] = dq.astype(BF16)
            dk = tn(ds, q4)
            dv = tn(pr.astype(BF16), do4)
            lo, hi = j * SEQ, (j + 1) * SEQ
            if not last:
                dk = s.dk[q, 0:nk, cols] + dk
                dv = s.dv[q, 0:nk, cols] + dv
            if j:
                s.dk[q, 0:nk, cols] = dk
                s.dv[q, 0:nk, cols] = dv
            s.dc[drows, D + g * STEP:D + (g + 1) * STEP] = dk[lo:hi].astype(BF16)
            s.dc[drows, 2 * D + g * STEP:2 * D + (g + 1) * STEP] = dv[lo:hi].astype(BF16)
    dc = s.dc[rows]
    da = jnp.concatenate([nt(dc, w.qkv[n:n + STEP, :]) for n in range(0, D, STEP)], 1)
    dx, dgain, dshift = norm_backward(da, p.gain(0), s.hat1.at[j], s.inv1.at[j])
    t.add(0, dgain)
    t.add(2, dshift)
    return dm1 + dx


def partner_copy(src, dst, sems):
    return pltpu.make_async_remote_copy(
        src_ref=src, dst_ref=dst, send_sem=sems.at[0], recv_sem=sems.at[1],
        device_id={"section": 1 - lax.axis_index("section")}, device_id_type=MESH)


def layers_kernel(tokens, out_grad, passes, embed, w_qkv, w_out, w_up, w_down, gains, biases, up_bias,
                  keep, give, a_o, o_o, b_o, e_o, dc_o, dz_o, df_o, dr_o, small,
                  qkv_v, out_v, up_v, down_v, q, k, v, prob, hat1, inv1, hat2, inv2, slope, do, dk, dv, state,
                  half_out, halves, leave, arrive, wsem, xsem, hsem):
    sec = lax.axis_index("section")
    loads = [pltpu.make_async_copy(src, dst, wsem.at[i]) for i, (src, dst) in enumerate(
        ((w_qkv.at[0], qkv_v), (w_out.at[0], out_v), (w_up.at[0], up_v), (w_down.at[0], down_v)))]
    for c in loads:
        c.start()
    half_out[...] = jnp.where(sec == 0, out_grad[...], tokens[...])
    own = jnp.where(sec == 0, tokens[...], out_grad[...])
    barrier = pltpu.get_barrier_semaphore()
    pl.semaphore_signal(barrier, inc=1, device_id={"section": 1 - sec}, device_id_type=MESH)
    pl.semaphore_wait(barrier, 1)
    exchange = partner_copy(half_out, halves.at[sec], xsem)
    exchange.start()
    halves[sec] = own

    w = Names(qkv=qkv_v, out=out_v, up=up_v, down=down_v)
    pending = set(range(4))

    def wait(i):
        if i in pending:
            pending.discard(i)
            loads[i].wait()
    w.wait = wait
    p = Names(gain=lambda i: gains[0, i:i + 1, :], bias=lambda i: biases[0, i:i + 1, :],
              up=lambda lo, hi: up_bias[:, lo:hi])
    s = Names(q=q, k=k, v=v, p=prob, hat1=hat1, inv1=inv1, hat2=hat2, inv2=inv2, slope=slope, do=do, dk=dk, dv=dv,
              a=a_o, o=o_o, b=b_o, e=e_o, dc=dc_o, dz=dz_o, df=df_o, dr=dr_o)
    small[...] = jnp.zeros_like(small)

    def add(i, value):
        small[i:i + 1, :] = small[i:i + 1, :] + value
    t = Names(add=add)
    k[...] = jnp.zeros_like(k)
    v[...] = jnp.zeros_like(v)
    row = lax.broadcasted_iota(jnp.int32, (R, 1), 0)
    count = jnp.where(row < SEQ, passes[0], passes[1]) - 1
    count = jnp.where(sec == 0, SLOTS, count)
    hand = partner_copy(leave, arrive, hsem)
    exchange.wait()

    def joined():
        parts = [halves[h, i] for i in range(2) for h in range(2)]
        return jnp.concatenate(parts, 0).astype(F32)

    @pl.when(sec == 0)
    def _():
        state[...] = joined()

    @pl.when(sec == 1)
    def _():
        hand.wait_recv()
        state[...] = arrive[...].astype(F32)

    def step_forward(j, row_of):
        h = state[...]
        r = forward(j, h + row_of, w, p, s)
        state[...] = jnp.where(count > j, r, h)

    def step_backward(j, last):
        g = state[...]
        du = backward(j, jnp.where(count > j, g, 0.0), w, p, s, t, last)
        add(8 + j, jnp.sum(du, 0, keepdims=True))
        state[...] = jnp.where(count > j, du, g)

    step_forward(0, jnp.where(sec == 0, embed[0:1, :], embed[1:2, :]))

    @pl.when(sec == 0)
    def _():
        leave[...] = state[...].astype(BF16)
        hand.start()
        for ref in (a_o, o_o, b_o, e_o, dc_o, dz_o, df_o, dr_o):
            ref[R:, :] = jnp.zeros((ROWS - R, ref.shape[1]), BF16)
        dk[:, 0:128] = jnp.zeros((2, 128, D), F32)
        dv[:, 0:128] = jnp.zeros((2, 128, D), F32)
        hand.wait()
        state[...] = arrive[...].astype(F32)

    @pl.when(sec == 1)
    def _():
        for j in range(1, SLOTS):
            step_forward(j, embed[j + 1:j + 2, :])
        final = state[...].astype(BF16)
        for i in range(2):
            give[i] = final[i * SEQ:i * SEQ + 32]
            keep[i] = final[i * SEQ + 32:i * SEQ + 64]
        state[...] = joined()
        for j in range(SLOTS - 1, 0, -1):
            step_backward(j, j == SLOTS - 1)

    step_backward(0, False)

    @pl.when(sec == 0)
    def _():
        final = state[...].astype(BF16)
        for i in range(2):
            keep[i] = final[i * SEQ:i * SEQ + 32]
            give[i] = final[i * SEQ + 32:i * SEQ + 64]

    @pl.when(sec == 1)
    def _():
        leave[...] = state[...].astype(BF16)
        hand.start()
        hand.wait_send()


def layers(*args):
    def shape(*dims, dtype=BF16):
        return jax.ShapeDtypeStruct(dims, dtype)
    vmem = pl.BlockSpec(memory_space=VM)
    hbm = pl.BlockSpec(memory_space=pl.ANY)
    return pl.pallas_call(
        layers_kernel,
        out_shape=[shape(2, 32, D), shape(2, 32, D), shape(ROWS, D), shape(ROWS, D), shape(ROWS, D), shape(ROWS, FF),
                   shape(ROWS, 3 * D), shape(ROWS, D), shape(ROWS, FF), shape(ROWS, D), shape(16, D, dtype=F32)],
        in_specs=[vmem, vmem, pl.BlockSpec(memory_space=pltpu.SMEM), vmem] + [hbm] * 4 + [vmem] * 3,
        out_specs=[vmem] * 11,
        scratch_shapes=[
            VM((D, 3 * D), BF16), VM((D, D), BF16), VM((D, FF), BF16), VM((FF, D), BF16),
            VM((SLOTS, R, D), BF16), VM((2, 256, D), BF16), VM((2, 256, D), BF16), VM((SLOTS, 6, 256, 256), F32),
            VM((SLOTS, R, D), F32), VM((SLOTS, R, 128), F32), VM((SLOTS, R, D), F32), VM((SLOTS, R, 128), F32),
            VM((SLOTS, R, FF), F32), VM((R, D), BF16), VM((2, 256, D), F32), VM((2, 256, D), F32), VM((R, D), F32),
            VM((2, 32, D), BF16), VM((2, 2, 32, D), BF16), VM((R, D), BF16), VM((R, D), BF16),
            pltpu.SemaphoreType.DMA((4,)), pltpu.SemaphoreType.DMA((2,)), pltpu.SemaphoreType.DMA((2,))],
        compiler_params=pltpu.CompilerParams(collective_id=0, has_side_effects=True, vmem_limit_bytes=62 * 2**20),
        name="layers",
    )(*args)


class Ring:
    def __init__(self, axis, half, near, far, send, recv, base):
        self.axis, self.half, self.near, self.far = axis, half, near, far
        self.send, self.recv, self.base = send, recv, base
        self.copies = {}

    def pos(self):
        return lax.rem(lax.div(lax.axis_index("dp"), STRIDE[self.axis]), 4)

    def at(self, by, half):
        return self.half(lax.rem(self.pos() + by, 4), half)

    def start(self, *slots):
        for slot in slots:
            by, half, dst, to = (
                (2, 0, self.far.at[0], 1), (2, 1, self.far.at[1], 3),
                (1, 1, self.near.at[0, 1], 1), (3, 0, self.near.at[1, 0], 3),
                (1, 0, self.near.at[0, 0], 1), (3, 1, self.near.at[1, 1], 3))[slot]
            copy = pltpu.make_async_remote_copy(
                src_ref=self.at(by, half), dst_ref=dst,
                send_sem=self.send.at[self.base + slot], recv_sem=self.recv.at[self.base + slot],
                device_id={"dp": neighbour(self.axis, to)}, device_id_type=MESH)
            copy.start()
            self.copies[slot] = copy

    def middle(self):
        self.copies[0].wait_recv()
        add_into(self.at(1, 0), self.far.at[0])
        self.start(4)
        self.copies[1].wait_recv()
        add_into(self.at(3, 1), self.far.at[1])
        self.start(5)

    def finish(self, store):
        for slot in (2, 3, 4, 5):
            self.copies[slot].wait_recv()
        for h in (0, 1):
            own = self.at(0, h)

            def body(idx, c, w):
                key = idx + (slice(None), slice(c, c + w))
                store(h, idx, c, w, own[key].astype(F32) + self.near.at[0, h][key].astype(F32)
                      + self.near.at[1, h][key].astype(F32))
            each(own, body)

    def drain(self):
        for copy in self.copies.values():
            copy.wait_send()


def neighbour(axis, by):
    dp = lax.axis_index("dp")
    pos = lax.rem(lax.div(dp, STRIDE[axis]), 4)
    return dp + (lax.rem(pos + by, 4) - pos) * STRIDE[axis]


def each(ref, body):
    lead, cols = ref.shape[:-2], ref.shape[-1]
    width = 768 if cols % 768 == 0 else cols
    count = int(np.prod(lead)) if lead else 1

    def at(i):
        idx = []
        for size in reversed(lead):
            idx.append(lax.rem(i, size) if not isinstance(i, int) else i % size)
            i = lax.div(i, size) if not isinstance(i, int) else i // size
        for c in range(0, cols, width):
            body(tuple(reversed(idx)), c, width)
    if count <= 4:
        for i in range(count):
            at(i)
    else:
        def step(i, carry):
            at(i)
            return carry
        lax.fori_loop(0, count, step, 0)


def add_into(dst, src):
    def body(idx, c, w):
        key = idx + (slice(None), slice(c, c + w))
        dst[key] = (dst[key].astype(F32) + src[key].astype(F32)).astype(BF16)
    each(dst, body)


def reduce_kernel(a, o, b, e, dc, dz, df, dr, small, q_out, o_out, u_out, d_out, small_out, up_out,
                  at_, ot, bt, et, qw, ow, uw, dw, *rest):
    bufs, (vec, vec_in, ups, ups_in, send, recv, ssend, srecv) = rest[:-8], rest[-8:]
    bufs = list(bufs)
    dp = lax.axis_index("dp")
    sec = lax.axis_index("section")
    barrier = pltpu.get_barrier_semaphore()
    for axis in STRIDE:
        for by in (1, 3):
            pl.semaphore_signal(barrier, inc=1, device_id={"dp": neighbour(axis, by)}, device_id_type=MESH)
    unit = (lax.broadcasted_iota(jnp.int32, (STEP, STEP), 0)
            == lax.broadcasted_iota(jnp.int32, (STEP, STEP), 1)).astype(BF16)

    def turned(dst, src):
        flat = dst.reshape(src.shape[1], ROWS)
        for n in range(0, src.shape[1], STEP):
            flat[n:n + STEP, :] = nt(unit, src[:, n:n + STEP]).astype(BF16)
    r = lax.broadcasted_iota(jnp.int32, (384, 384), 0)
    c = lax.broadcasted_iota(jnp.int32, (384, 384), 1)
    within = lax.rem(r, 192)
    source = r - within + lax.rem(lax.div(within, 12), 4) * 48 + lax.div(within, 48) * 12 + lax.rem(within, 12)
    order = (c == source).astype(BF16)
    turned(et, e)
    bflat = bt.reshape(D, ROWS)
    for n in (0, 384):
        bflat[n:n + 384, :] = nt(order, b[:, n:n + 384]).astype(BF16)
    turned(at_, a)
    turned(ot, o)
    pl.semaphore_wait(barrier, 6)

    base = [0]

    def ring(axis, half):
        made = Ring(axis, half, bufs.pop(0), bufs.pop(0), send, recv, base[0])
        base[0] += 6
        return made

    d1 = ring("z", lambda i, h: dw.at[pl.ds(2 * h, 2), :, i])
    u1 = ring("y", lambda i, h: uw.at[i, pl.ds(2 * h, 2)])
    q1 = ring("x", lambda i, h: qw.at[pl.ds(2 * h, 2), i])
    o1 = ring("x", lambda i, h: ow.at[pl.ds(2 * h, 2), i])

    def d_block(i):
        def one(y, carry):
            dw[y, :, i] = nn(et[y, :, i].reshape(192, ROWS), dr[...]).astype(BF16).reshape(4, 48, D)
            return carry
        lax.fori_loop(0, 4, one, 0)

    def u_block(i):
        for n in range(0, FF, D):
            uw[i, :, :, n:n + D] = nn(bt[i].reshape(192, ROWS), df[:, n:n + D]).astype(BF16).reshape(4, 48, D)

    def q_block(i):
        for n in range(0, 3 * D, D):
            qw[:, i, :, n:n + D] = nn(at_[:, i].reshape(192, ROWS), dc[:, n:n + D]).astype(BF16).reshape(4, 48, D)

    def o_block(i):
        ow[:, i] = nn(ot[:, i].reshape(192, ROWS), dz[...]).astype(BF16).reshape(4, 48, D)

    first = ((d1, d_block), (u1, u_block), (q1, q_block), (o1, o_block))
    for by, slots in ((2, (0, 1)), (1, (2,)), (3, (3,)), (0, ())):
        for one, block in first:
            block(lax.rem(one.pos() + by, 4))
            one.start(*slots)

    line = jnp.ones((8, ROWS), BF16)
    vec[0] = small[...]

    def put(i, value):
        vec[0, i:i + 1, :] = value[0:1]
    put(2 + 1, nn(line, dc[:, 0:D]))
    put(2 + 2, nn(line, dc[:, 2 * D:3 * D]))
    put(2 + 3, nn(line, dz[...]))
    put(2 + 5, nn(line, dr[...]))
    for i in range(4):
        put(12 + i, nn(line, df[:, i * D:(i + 1) * D]))
    swaps = []

    def swap_start():
        i = len(swaps)
        axis = ("y", "x", "z")[i // 2]
        pos = lax.rem(lax.div(dp, STRIDE[axis]), 4)
        peer = pos + 1 - 2 * lax.rem(pos, 2) if i % 2 == 0 else 3 - pos
        copy = pltpu.make_async_remote_copy(
            src_ref=vec.at[i], dst_ref=vec_in.at[i], send_sem=ssend.at[i], recv_sem=srecv.at[i],
            device_id={"dp": dp + (peer - pos) * STRIDE[axis]}, device_id_type=MESH)
        copy.start()
        swaps.append(copy)

    def swap_next():
        i = len(swaps) - 1
        swaps[-1].wait_recv()
        vec[i + 1] = vec[i] + vec_in[i]
        if i < 5:
            swap_start()
    swap_start()

    d2s, u2s, q2s, o2s, d3s, u3s, q3s, o3s = [bufs.pop() for _ in range(8)][::-1]
    d2 = ring("x", lambda i, h: d2s.at[pl.ds(2 * h, 2), i])
    u2 = ring("z", lambda i, h: u2s.at[i, :, pl.ds(1536 * h, 1536)])
    q2 = ring("y", lambda i, h: q2s.at[i, :, pl.ds(1152 * h, 1152)])
    o2 = ring("y", lambda i, h: o2s.at[i, :, pl.ds(384 * h, 384)])
    d3 = ring("y", lambda i, h: d3s.at[i, :, pl.ds(384 * h, 384)])
    u3 = ring("x", lambda i, h: u3s.at[i, :, pl.ds(1536 * h, 1536)])
    q3 = ring("z", lambda i, h: q3s.at[i, :, pl.ds(1152 * h, 1152)])
    o3 = ring("z", lambda i, h: o3s.at[i, :, pl.ds(384 * h, 384)])

    def to_rows(dst):
        def store(h, idx, c, w, value):
            dst[(idx[0] + 2 * h,) + idx[1:] + (slice(None), slice(c, c + w))] = value.astype(BF16)
        return store

    def to_twelfths(dst):
        width = dst.shape[-1] // 2

        def store(h, idx, c, w, value):
            for i in range(4):
                rows = jnp.concatenate([value[12 * i:12 * i + 12], jnp.zeros((4, w), F32)], 0)
                dst[i, :, width * h + c:width * h + c + w] = rows.astype(BF16)
        return store

    def to_out(dst):
        rows, width = dst.shape[0], dst.shape[1] // 2

        def store(h, idx, c, w, value):
            dst[:, width * h + c:width * h + c + w] = value[:rows]
        return store

    everything = (0, 1, 2, 3)
    for one in (d1, u1, q1, o1):
        one.middle()
    swap_next()
    for one, store, following in ((d1, to_rows(d2s), d2), (u1, to_rows(u2s), u2),
                                  (q1, to_rows(q2s), q2), (o1, to_rows(o2s), o2)):
        one.finish(store)
        following.start(*everything)
    swap_next()
    for one in (d2, u2, q2, o2):
        one.middle()
    swap_next()
    for one, store, following in ((d2, to_rows(d3s), d3), (u2, to_twelfths(u3s), u3),
                                  (q2, to_twelfths(q3s), q3), (o2, to_twelfths(o3s), o3)):
        one.finish(store)
        following.start(*everything)
    swap_next()
    for one in (d3, u3, q3, o3):
        one.middle()
    swap_next()
    for one, dst in ((d3, d_out), (u3, u_out), (q3, q_out), (o3, o_out)):
        one.finish(to_out(dst))
    swap_next()
    small_out[...] = vec[6]
    for one in (d1, u1, q1, o1, d2, u2, q2, o2, d3, u3, q3, o3):
        one.drain()
    for copy in swaps:
        copy.wait_send()


def reduce(*args):
    def ring(*shape):
        return [VM((2, 2) + shape, BF16), VM((2,) + shape, BF16)]
    dma = pltpu.SemaphoreType.DMA
    return pl.pallas_call(
        reduce_kernel,
        out_shape=[jax.ShapeDtypeStruct(dims, F32) for dims in (
            (12, 3 * D), (12, D), (12, FF), (48, D), (16, D), (8, 128))],
        in_specs=[pl.BlockSpec(memory_space=VM)] * 9,
        out_specs=[pl.BlockSpec(memory_space=VM)] * 6,
        scratch_shapes=[
            VM((4, 4, 48, ROWS), BF16), VM((4, 4, 48, ROWS), BF16), VM((4, 4, 48, ROWS), BF16),
            VM((4, 4, 4, 48, ROWS), BF16),
            VM((4, 4, 48, 3 * D), BF16), VM((4, 4, 48, D), BF16), VM((4, 4, 48, FF), BF16),
            VM((4, 4, 4, 48, D), BF16)]
        + ring(2, 4, 48, D) + ring(2, 48, FF) + ring(2, 48, 3 * D) + ring(2, 48, D)
        + ring(2, 48, D) + ring(48, FF // 2) + ring(48, 1152) + ring(48, 384)
        + ring(48, 384) + ring(16, FF // 2) + ring(16, 1152) + ring(16, 384)
        + [VM((4, 4, 48, D), BF16), VM((4, 48, FF), BF16), VM((4, 48, 3 * D), BF16), VM((4, 48, D), BF16),
           VM((4, 48, D), BF16), VM((4, 16, FF), BF16), VM((4, 16, 3 * D), BF16), VM((4, 16, D), BF16),
           VM((7, 16, D), F32), VM((6, 16, D), F32), VM((8, 128), F32), VM((8, 128), F32),
           dma((72,)), dma((72,)), dma((6,)), dma((6,))],
        compiler_params=pltpu.CompilerParams(collective_id=1, has_side_effects=True, vmem_limit_bytes=62 * 2**20),
        name="reduce",
    )(*args)


def local(tokens, out_grad, passes, embed, w_qkv, w_out, w_up, w_down, gains, biases, up_bias):
    sec = lax.axis_index("section")
    dp = lax.axis_index("dp")
    keep, give, a, o, b, e, dc, dz, df, dr, small = layers(
        tokens, out_grad, passes, embed, w_qkv, w_out, w_up, w_down, gains, biases, up_bias)
    g_qkv, g_out, g_up, g_down, sums, _ = reduce(a, o, b, e, dc, dz, df, dr, small)
    give, sums = lax.optimization_barrier((give, sums))
    swap = [(0, 1), (1, 0)]
    got = lax.ppermute(give, "section", swap)
    slot_sums = sums[8:12]
    other_sums = lax.ppermute(slot_sums, "section", swap)
    hidden_out = jnp.where(sec == 0, got, keep)
    token_grad = jnp.where(sec == 0, keep, got)
    first = jnp.where(sec == 0, slot_sums, other_sums)[0:1]
    later = jnp.where(sec == 0, other_sums, slot_sums)
    embed_sums = jnp.concatenate([first, later], 0)
    g_gains = lax.dynamic_slice(sums[0:2], (0, dp * 12), (2, 12))
    g_bias = lax.dynamic_slice(sums[2:8], (0, dp * 12), (6, 12))
    g_up_bias = lax.dynamic_slice(sums[12:16].reshape(FF), (dp * 48,), (48,))
    g_embed = lax.dynamic_slice(embed_sums, (0, (sec * 64 + dp) * 6), (5, 6))
    return (hidden_out, token_grad, g_qkv[None], g_out[None], g_up[None], g_down[None],
            g_gains[None], g_bias[None], g_up_bias[None], g_embed)


def solution(mesh):
    split = ("section",)
    placed = (
        P("dp", "section", None), P("dp", "section", None), P("dp"), P(),
        P("section", None, None), P("section", None, None), P("section", None, None), P("section", None, None),
        P("section", None, None), P("section", None, None), P("section", None))
    return jax.shard_map(
        local, mesh=mesh, in_specs=placed,
        out_specs=(
            P("dp", "section", None), P("dp", "section", None),
            P("section", "dp", None), P("section", "dp", None), P("section", "dp", None), P("section", "dp", None),
            P("section", None, "dp"), P("section", None, "dp"), P("section", "dp"), P(None, ("section", "dp"))),
        check_vma=False)
```

```python
import jax
import jax.numpy as jnp
import numpy as np
from jax import lax
from jax.experimental import pallas as pl
from jax.experimental.pallas import tpu as pltpu
from jax.sharding import PartitionSpec as P

F32 = jnp.float32
BF16 = jnp.bfloat16
VM = pltpu.VMEM
MESH = pl.DeviceIdType.MESH
D = 768
FF = 3072
SEQ = 64
R = 2 * SEQ
SLOTS = 4
ROWS = SLOTS * R
STEP = 256
STRIDE = {"y": 16, "x": 4, "z": 1}
Q, U, W = 0, 1, 2
AXES = ("x", "z", "y")


class Names:
    def __init__(self, **entries):
        self.__dict__.update(entries)


def nn(a, b):
    return jnp.dot(a, b, preferred_element_type=F32)


def nt(a, b):
    return lax.dot_general(a, b, (((1,), (1,)), ((), ())), preferred_element_type=F32)


def tn(a, b):
    return lax.dot_general(a, b, (((0,), (0,)), ((), ())), preferred_element_type=F32)


def lane_masks(value, dtype):
    lane = lax.broadcasted_iota(jnp.int32, (1, STEP), 1) // 64
    return [jnp.where(lane == h, value, 0.0).astype(dtype) for h in range(4)]


def norm_forward(u, gain, shift, hat_ref, inv_ref):
    out = []
    for r in range(0, R, 32):
        v = u[r:r + 32]
        centre = v - jnp.sum(v, -1, keepdims=True) * (1.0 / D)
        inv = lax.rsqrt(jnp.sum(centre * centre, -1, keepdims=True) * (1.0 / D) + 1e-5)
        hat = centre * inv
        hat_ref[r:r + 32] = hat
        inv_ref[r:r + 32] = jnp.broadcast_to(inv, (32, 128))
        out.append((hat * gain + shift).astype(BF16))
    return jnp.concatenate(out, 0)


def norm_backward(dy, gain, hat_ref, inv_ref):
    out, dgain, dshift = [], 0.0, 0.0
    for r in range(0, R, 32):
        g = dy[r:r + 32]
        hat = hat_ref[r:r + 32]
        inv = inv_ref[r:r + 32][:, :1]
        dgain = dgain + jnp.sum(g * hat, 0, keepdims=True)
        dshift = dshift + jnp.sum(g, 0, keepdims=True)
        gg = g * gain
        m1 = jnp.sum(gg, -1, keepdims=True) * (1.0 / D)
        m2 = jnp.sum(gg * hat, -1, keepdims=True) * (1.0 / D)
        out.append((gg - m1 - hat * m2) * inv)
    return jnp.concatenate(out, 0), dgain, dshift


def keys_of(j):
    return 128 if j < 2 else 256


def forward(j, u, w, p, s):
    rows = slice(j * R, (j + 1) * R)
    a = norm_forward(u, p.gain(0), p.bias(0), s.hat1.at[j], s.inv1.at[j])
    s.ao[0, rows] = a
    w.wait(0)
    for n in range(0, 3 * D, STEP):
        c = nn(a, w.qkv[:, n:n + STEP])
        k = n % D
        if n < D:
            s.q[j, :, k:k + STEP] = (c + p.bias(1)[:, k:k + STEP]).astype(BF16)
        elif n < 2 * D:
            c = c.astype(BF16)
            for q in range(2):
                s.k[q, j * SEQ:(j + 1) * SEQ, k:k + STEP] = c[q * SEQ:(q + 1) * SEQ]
        else:
            c = (c + p.bias(2)[:, k:k + STEP]).astype(BF16)
            for q in range(2):
                s.v[q, j * SEQ:(j + 1) * SEQ, k:k + STEP] = c[q * SEQ:(q + 1) * SEQ]
    nk = keys_of(j)
    ones = lane_masks(1.0, F32)
    eighth = lane_masks(0.125, BF16)
    col = lax.broadcasted_iota(jnp.int32, (SEQ, nk), 1)
    row = lax.broadcasted_iota(jnp.int32, (SEQ, nk), 0)
    allow = ((col & 63) <= row) & (col < (j + 1) * SEQ)
    veto = jnp.where(allow, 0.0, -1e30)
    veto = jnp.concatenate([veto] * 4, 0)
    for q in range(2):
        qrows = slice(q * SEQ, (q + 1) * SEQ)
        for g in range(3):
            cols = slice(g * STEP, (g + 1) * STEP)
            q4 = s.q[j, qrows, cols]
            q4 = jnp.concatenate([q4 * m for m in eighth], 0)
            sc = nt(q4, s.k[q, 0:nk, cols]) + veto
            ex = jnp.exp(sc - jnp.max(sc, -1, keepdims=True))
            pr = ex * (1.0 / jnp.sum(ex, -1, keepdims=True))
            s.p[j, 3 * q + g, :, 0:nk] = pr
            o4 = nn(pr.astype(BF16), s.v[q, 0:nk, cols])
            o = sum(o4[h * SEQ:(h + 1) * SEQ] * ones[h] for h in range(4))
            s.ao[1, j * R + q * SEQ:j * R + (q + 1) * SEQ, cols] = o.astype(BF16)
    s.post(0, Q, j)
    o = s.ao[1, rows]
    w.wait(1)
    m1 = u + (jnp.concatenate([nn(o, w.out[:, n:n + STEP]) for n in range(0, D, STEP)], 1) + p.bias(3))
    b = norm_forward(m1, p.gain(1), p.bias(4), s.hat2.at[j], s.inv2.at[j])
    s.b[rows] = b
    s.post(0, U, j)
    w.wait(2)
    for n in range(0, FF, STEP):
        f = nn(b, w.up[:, n:n + STEP]) + p.up(n, n + STEP)
        t = jnp.tanh(0.7978845608 * (f + 0.044715 * f * f * f))
        half = 0.5 * (1.0 + t)
        s.e[rows, n:n + STEP] = (f * half).astype(BF16)
        s.slope[j, :, n:n + STEP] = half + 0.5 * f * (1.0 - t * t) * (
            0.7978845608 + 0.7978845608 * 3 * 0.044715 * f * f)
    s.post(0, W, j)
    e = s.e[rows]
    w.wait(3)
    r = jnp.concatenate([nn(e, w.down[:, n:n + STEP]) for n in range(0, D, STEP)], 1)
    return m1 + (r + p.bias(5))


def backward(j, dr, w, p, s, t, last):
    rows = slice(j * R, (j + 1) * R)
    dr2 = dr.astype(BF16)
    s.dr[rows] = dr2
    s.post(1, W, j)
    t.add(2 + 5, jnp.sum(dr, 0, keepdims=True))
    for n in range(0, FF, STEP):
        de = nt(dr2, w.down[n:n + STEP, :])
        df = s.slope[j, :, n:n + STEP] * de
        t.add(12 + n // D, jnp.sum(df, 0, keepdims=True), n % D)
        s.df[rows, n:n + STEP] = df.astype(BF16)
    s.post(1, U, j)
    df = s.df[rows]
    db = jnp.concatenate([nt(df, w.up[n:n + STEP, :]) for n in range(0, D, STEP)], 1)
    dm, dgain, dshift = norm_backward(db, p.gain(1), s.hat2.at[j], s.inv2.at[j])
    t.add(1, dgain)
    t.add(2 + 4, dshift)
    dm1 = dr + dm
    dz = dm1.astype(BF16)
    s.dcz[rows, 3 * D:] = dz
    t.add(2 + 3, jnp.sum(dm1, 0, keepdims=True))
    for n in range(0, D, STEP):
        s.do[:, n:n + STEP] = nt(dz, w.out[n:n + STEP, :]).astype(BF16)
    nk = keys_of(j)
    ones = lane_masks(1.0, BF16)
    eighth = lane_masks(0.125, BF16)
    eighth32 = lane_masks(0.125, F32)
    for q in range(2):
        qrows = slice(q * SEQ, (q + 1) * SEQ)
        drows = slice(j * R + q * SEQ, j * R + (q + 1) * SEQ)
        for g in range(3):
            cols = slice(g * STEP, (g + 1) * STEP)
            do4 = s.do[qrows, cols]
            do4 = jnp.concatenate([do4 * m for m in ones], 0)
            q4 = s.q[j, qrows, cols]
            q4 = jnp.concatenate([q4 * m for m in eighth], 0)
            dp = nt(do4, s.v[q, 0:nk, cols])
            pr = s.p[j, 3 * q + g, :, 0:nk]
            ds = (pr * (dp - jnp.sum(pr * dp, -1, keepdims=True))).astype(BF16)
            dq4 = nn(ds, s.k[q, 0:nk, cols])
            dq = sum(dq4[h * SEQ:(h + 1) * SEQ] * eighth32[h] for h in range(4))
            t.add(2 + 1, jnp.sum(dq, 0, keepdims=True), g * STEP)
            s.dcz[drows, cols] = dq.astype(BF16)
            dk = tn(ds, q4)
            dv = tn(pr.astype(BF16), do4)
            lo, hi = j * SEQ, (j + 1) * SEQ
            if not last:
                dk = s.dk[q, 0:nk, cols] + dk
                dv = s.dv[q, 0:nk, cols] + dv
            if j:
                s.dk[q, 0:nk, cols] = dk
                s.dv[q, 0:nk, cols] = dv
            s.dcz[drows, D + g * STEP:D + (g + 1) * STEP] = dk[lo:hi].astype(BF16)
            s.dcz[drows, 2 * D + g * STEP:2 * D + (g + 1) * STEP] = dv[lo:hi].astype(BF16)
            t.add(2 + 2, jnp.sum(dv[lo:hi], 0, keepdims=True), g * STEP)
    s.post(1, Q, j)
    dc = s.dcz[rows, 0:3 * D]
    da = jnp.concatenate([nt(dc, w.qkv[n:n + STEP, :]) for n in range(0, D, STEP)], 1)
    dx, dgain, dshift = norm_backward(da, p.gain(0), s.hat1.at[j], s.inv1.at[j])
    t.add(0, dgain)
    t.add(2, dshift)
    return dm1 + dx


def partner_copy(src, dst, sems):
    return pltpu.make_async_remote_copy(
        src_ref=src, dst_ref=dst, send_sem=sems.at[0], recv_sem=sems.at[1],
        device_id={"section": 1 - lax.axis_index("section")}, device_id_type=MESH)


class Ring:
    def __init__(self, axis, half, near, far, send, recv, base):
        self.axis, self.half, self.near, self.far = axis, half, near, far
        self.send, self.recv, self.base = send, recv, base
        self.copies = {}

    def pos(self):
        return lax.rem(lax.div(lax.axis_index("dp"), STRIDE[self.axis]), 4)

    def at(self, by, half):
        return self.half(lax.rem(self.pos() + by, 4), half)

    def start(self, *slots):
        for slot in slots:
            by, half, dst, to = (
                (2, 0, self.far.at[0], 1), (2, 1, self.far.at[1], 3),
                (1, 1, self.near.at[0, 1], 1), (3, 0, self.near.at[1, 0], 3),
                (1, 0, self.near.at[0, 0], 1), (3, 1, self.near.at[1, 1], 3))[slot]
            copy = pltpu.make_async_remote_copy(
                src_ref=self.at(by, half), dst_ref=dst,
                send_sem=self.send.at[self.base + slot], recv_sem=self.recv.at[self.base + slot],
                device_id={"dp": neighbour(self.axis, to)}, device_id_type=MESH)
            copy.start()
            self.copies[slot] = copy

    def middle(self):
        self.copies[0].wait_recv()
        add_into(self.at(1, 0), self.far.at[0])
        self.start(4)
        self.copies[1].wait_recv()
        add_into(self.at(3, 1), self.far.at[1])
        self.start(5)

    def finish(self, store):
        for slot in (2, 3, 4, 5):
            self.copies[slot].wait_recv()
        for h in (0, 1):
            own = self.at(0, h)

            def body(idx, c, w):
                key = idx + (slice(None), slice(c, c + w))
                store(h, idx, c, w, own[key].astype(F32) + self.near.at[0, h][key].astype(F32)
                      + self.near.at[1, h][key].astype(F32))
            each(own, body)

    def drain(self):
        for copy in self.copies.values():
            copy.wait_send()


def neighbour(axis, by):
    dp = lax.axis_index("dp")
    pos = lax.rem(lax.div(dp, STRIDE[axis]), 4)
    return dp + (lax.rem(pos + by, 4) - pos) * STRIDE[axis]


def each(ref, body):
    lead, cols = ref.shape[:-2], ref.shape[-1]
    width = 768 if cols % 768 == 0 else cols
    count = int(np.prod(lead)) if lead else 1

    def at(i):
        idx = []
        for size in reversed(lead):
            idx.append(lax.rem(i, size) if not isinstance(i, int) else i % size)
            i = lax.div(i, size) if not isinstance(i, int) else i // size
        for c in range(0, cols, width):
            body(tuple(reversed(idx)), c, width)
    if count <= 4:
        for i in range(count):
            at(i)
    else:
        def step(i, carry):
            at(i)
            return carry
        lax.fori_loop(0, count, step, 0)


def add_into(dst, src):
    def body(idx, c, w):
        key = idx + (slice(None), slice(c, c + w))
        dst[key] = (dst[key].astype(F32) + src[key].astype(F32)).astype(BF16)
    each(dst, body)


def rank(axis):
    return lax.rem(lax.div(lax.axis_index("dp"), STRIDE[axis]), 4)


def main_kernel(tokens, out_grad, passes, embed, w_qkv, w_out, w_up, w_down, gains, biases, up_bias,
                keep, got, q_out, o_out, u_out, d_out, sums, sums_other, xs, ys,
                qkv_v, out_v, up_v, down_v, q, k, v, prob, hat1, inv1, hat2, inv2, slope, do, dk, dv, state,
                ao, b, e, dcz, df, dr, small, half_out, halves, leave, arrive, give,
                q2s, u2s, d2s, q3s, u3s, d3s, q2n, q2f, u2n, u2f, d2n, d2f, q3n, q3f, u3n, u3f, d3n, d3f,
                q4s, u4s, q4r, u4r, vec, vec_in,
                wsem, xsem, hsem, gsem, psem, vsem, psend, precv, plocal, stage, rsend, rrecv, asend, arecv, ssend, srecv):
    sec = lax.axis_index("section")
    dp = lax.axis_index("dp")
    loads = [pltpu.make_async_copy(src, dst, wsem.at[i]) for i, (src, dst) in enumerate(
        ((w_qkv.at[0], qkv_v), (w_out.at[0], out_v), (w_up.at[0], up_v), (w_down.at[0], down_v)))]
    for c in loads:
        c.start()
    ranks = [rank(axis) for axis in AXES]
    peers = [[lax.rem(ranks[g] + by, 4) for by in range(4)] for g in range(3)]
    places = [[dp + (peers[g][by] - ranks[g]) * STRIDE[AXES[g]] for by in range(4)] for g in range(3)]
    offsets = [[pl.multiple_of(peers[g][by] * D, D) for by in range(4)] for g in range(3)]
    seconds = [lax.div(peers[Q][by], 3) for by in range(4)]
    barrier = pltpu.get_barrier_semaphore()
    for g in range(3):
        for by in (1, 2, 3):
            pl.semaphore_signal(barrier, inc=1, device_id={"dp": places[g][by]}, device_id_type=MESH)
            pl.semaphore_signal(barrier, inc=1, device_id={"dp": places[g][by], "section": 1 - sec},
                                device_id_type=MESH)
    pl.semaphore_signal(barrier, inc=1, device_id={"section": 1 - sec}, device_id_type=MESH)
    half_out[...] = jnp.where(sec == 0, out_grad[...], tokens[...])
    own = jnp.where(sec == 0, tokens[...], out_grad[...])
    pl.semaphore_wait(barrier, 19)
    exchange = partner_copy(half_out, halves.at[sec], xsem)
    exchange.start()
    halves[sec] = own

    landing = (xs, ys)
    local, remote = {}, {}
    for j in range(SLOTS):
        rows = pl.ds(j * R, R)
        for g in range(3):
            for which in range(2):
                for by in range(4):
                    if g == Q:
                        src = (ao.at[seconds[by], rows] if which == 0 else dcz.at[rows, pl.ds(offsets[g][by], D)])
                    elif g == U:
                        src = b.at[rows] if which == 0 else df.at[rows, pl.ds(offsets[g][by], D)]
                    else:
                        src = e.at[rows, pl.ds(offsets[g][by], D)] if which == 0 else dr.at[rows]
                    dst = landing[which].at[g, j, ranks[g]]
                    if by == 0 and j == 0:
                        local[which, g] = pltpu.make_async_copy(src, dst, plocal.at[which, g])
                        continue
                    remote[which, g, j, by] = pltpu.make_async_remote_copy(
                        src_ref=src, dst_ref=dst, send_sem=psend.at[which, g, j, by],
                        recv_sem=precv.at[which, g, j, ranks[g]],
                        device_id={"dp": places[g][by], "section": sec if j == 0 else 1 - sec},
                        device_id_type=MESH)

    def post(which, g, j):
        if j == 0:
            local[which, g].start()
        for by in (1, 2, 3, 0):
            if (which, g, j, by) in remote:
                remote[which, g, j, by].start()

    def arrived(which, g, j, by):
        there = landing[which].at[g, j, peers[g][by]]
        pltpu.make_async_remote_copy(
            src_ref=there, dst_ref=there, send_sem=psend.at[which, g, 0, 0],
            recv_sem=precv.at[which, g, j, peers[g][by]],
            device_id={"dp": places[g][1]}, device_id_type=MESH).wait_recv()

    def staged(g, j):
        copies = []
        for which, dst in ((0, e), (1, df)):
            for i in range(4):
                copies.append(pltpu.make_async_copy(
                    landing[which].at[g, j, i], dst.at[pl.ds((1 + g) * R, R), pl.ds(i * D, D)],
                    stage.at[which, g, i]))
        for c in copies:
            c.start()
        for c in copies:
            c.wait()

    def tall(ref, g, lo):
        rows = slice((1 + g) * R, (2 + g) * R)
        return jnp.concatenate([ref[rows, i * D + lo:i * D + lo + STEP] for i in range(4)], 0)

    def product(g, m, n):
        return tn(tall(e, g, m * STEP), tall(df, g, n * STEP))

    class Sum:
        def __init__(self, g, m, n):
            if g < 2:
                i = g * 9 + m * 3 + n
                self.refs = [prob.at[1 + i // 6, i % 6]]
            else:
                self.refs = [slope.at[1 + m, :, pl.ds((2 * n + h) * STEP, STEP)] for h in range(2)]

        def read(self):
            return jnp.concatenate([r[...] for r in self.refs], 0)

        def write(self, value):
            size = STEP // len(self.refs)
            for i, r in enumerate(self.refs):
                r[...] = value[i * size:(i + 1) * size]

    tiles = [(m, n) for m in range(3) for n in range(3)]
    second = {Q: q2s.reshape(D, D), U: u2s.reshape(D, D), W: d2s.reshape(D, D)}

    w = Names(qkv=qkv_v, out=out_v, up=up_v, down=down_v)
    pending = set(range(4))

    def wait(i):
        if i in pending:
            pending.discard(i)
            loads[i].wait()
    w.wait = wait
    p = Names(gain=lambda i: gains[0, i:i + 1, :], bias=lambda i: biases[0, i:i + 1, :],
              up=lambda lo, hi: up_bias[:, lo:hi])
    s = Names(q=q, k=k, v=v, p=prob, hat1=hat1, inv1=inv1, hat2=hat2, inv2=inv2, slope=slope, do=do, dk=dk, dv=dv,
              ao=ao, b=b, e=e, dcz=dcz, df=df, dr=dr, post=post)
    small[...] = jnp.zeros_like(small)

    def add(i, value, at=0):
        cols = slice(at, at + value.shape[1])
        small[i:i + 1, cols] = small[i:i + 1, cols] + value
    t = Names(add=add)
    k[...] = jnp.zeros_like(k)
    v[...] = jnp.zeros_like(v)
    row = lax.broadcasted_iota(jnp.int32, (R, 1), 0)
    count = jnp.where(row < SEQ, passes[0], passes[1]) - 1
    count = jnp.where(sec == 0, SLOTS, count)
    hand = partner_copy(leave, arrive, hsem)
    present = partner_copy(give, got, gsem)
    partial = [partner_copy(r, r, psem.at[i]) for i, r in enumerate((q2s, u2s, d2s))]
    exchange.wait()

    def joined():
        return jnp.concatenate([halves[h, i] for i in range(2) for h in range(2)], 0).astype(F32)

    @pl.when(sec == 0)
    def _():
        state[...] = joined()

    @pl.when(sec == 1)
    def _():
        hand.wait_recv()
        state[...] = arrive[...].astype(F32)

    def step_forward(j, row_of):
        h = state[...]
        r = forward(j, h + row_of, w, p, s)
        state[...] = jnp.where(count > j, r, h)

    def step_backward(j, last):
        g = state[...]
        du = backward(j, jnp.where(count > j, g, 0.0), w, p, s, t, last)
        add(8 + j, jnp.sum(du, 0, keepdims=True))
        state[...] = jnp.where(count > j, du, g)

    step_forward(0, jnp.where(sec == 0, embed[0:1, :], embed[1:2, :]))

    @pl.when(sec == 0)
    def _():
        leave[...] = state[...].astype(BF16)
        hand.start()
        dk[:, 0:128] = jnp.zeros((2, 128, D), F32)
        dv[:, 0:128] = jnp.zeros((2, 128, D), F32)
        for g in range(3):
            for m, n in tiles:
                Sum(g, m, n).write(jnp.zeros((STEP, STEP), F32))

        def slot(i, carry):
            j = SLOTS - 1 - i
            for g in (W, U, Q):
                for which in range(2):
                    for by in range(4):
                        arrived(which, g, j, by)
                staged(g, j)
                for m, n in tiles:
                    held = Sum(g, m, n)
                    held.write(held.read() + product(g, m, n))
            return carry
        lax.fori_loop(0, SLOTS - 1, slot, 0)
        for g in (W, U, Q):
            for m, n in tiles:
                second[g][m * STEP:(m + 1) * STEP, n * STEP:(n + 1) * STEP] = Sum(g, m, n).read().astype(BF16)
            partial[g].start()
        hand.wait()
        state[...] = arrive[...].astype(F32)

    @pl.when(sec == 1)
    def _():
        for j in range(1, SLOTS):
            step_forward(j, embed[j + 1:j + 2, :])
        final = state[...].astype(BF16)
        for i in range(2):
            give[i] = final[i * SEQ:i * SEQ + 32]
            keep[i] = final[i * SEQ + 32:i * SEQ + 64]
        present.start()
        state[...] = joined()
        for j in range(SLOTS - 1, 0, -1):
            step_backward(j, j == SLOTS - 1)

    step_backward(0, False)

    @pl.when(sec == 0)
    def _():
        final = state[...].astype(BF16)
        for i in range(2):
            keep[i] = final[i * SEQ:i * SEQ + 32]
            give[i] = final[i * SEQ + 32:i * SEQ + 64]
        present.start()
        for g in range(3):
            partial[g].wait_send()

    @pl.when(sec == 1)
    def _():
        leave[...] = state[...].astype(BF16)
        hand.start()
        for key, copy in remote.items():
            if key[2] > 0:
                copy.wait_send()

    swaps = []

    def swap_start():
        i = len(swaps)
        axis = ("y", "x", "z")[i // 2]
        pos = rank(axis)
        peer = pos + 1 - 2 * lax.rem(pos, 2) if i % 2 == 0 else 3 - pos
        copy = pltpu.make_async_remote_copy(
            src_ref=vec.at[i], dst_ref=vec_in.at[i], send_sem=ssend.at[i], recv_sem=srecv.at[i],
            device_id={"dp": dp + (peer - pos) * STRIDE[axis]}, device_id_type=MESH)
        copy.start()
        swaps.append(copy)

    def swap_next():
        i = len(swaps) - 1
        swaps[-1].wait_recv()
        vec[i + 1] = vec[i] + vec_in[i]
        if i < 5:
            swap_start()
    vec[0] = small[...]
    swap_start()

    base = [0]

    def ring(axis, half, near, far):
        made = Ring(axis, half, near, far, rsend, rrecv, base[0])
        base[0] += 6
        return made

    def by_columns(ref):
        return lambda i, h: ref.at[i, :, pl.ds(D // 2 * h, D // 2)]
    d2 = ring("z", lambda i, h: d2s.at[pl.ds(2 * h, 2), i], d2n, d2f)
    u2 = ring("x", lambda i, h: u2s.at[pl.ds(2 * h, 2), i], u2n, u2f)
    q2 = ring("y", by_columns(q2s), q2n, q2f)
    d3 = ring("x", by_columns(d3s), d3n, d3f)
    u3 = ring("y", by_columns(u3s), u3n, u3f)
    q3 = ring("z", by_columns(q3s), q3n, q3f)

    everything = (0, 1, 2, 3)
    for g, one in ((W, d2), (U, u2), (Q, q2)):
        for which in range(2):
            local[which, g].wait()
            for by in (1, 2, 3):
                arrived(which, g, 0, by)
        staged(g, 0)

        @pl.when(sec == 1)
        def _():
            partial[g].wait_recv()
        for m, n in tiles:
            part = second[g].at[m * STEP:(m + 1) * STEP, n * STEP:(n + 1) * STEP]
            held = jnp.where(sec == 1, part[...].astype(F32), 0.0)
            part[...] = (held + product(g, m, n)).astype(BF16)
        one.start(*everything)

    def to_rows(dst):
        def store(h, idx, c, w, value):
            dst[(idx[0] + 2 * h,) + idx[1:] + (slice(None), slice(c, c + w))] = value.astype(BF16)
        return store

    def to_groups(dst):
        def store(h, idx, c, w, value):
            lo = D // 2 * h + c
            for i in range(4):
                rows = jnp.concatenate([value[48 * x + 12 * i:48 * x + 12 * i + 12] for x in range(4)], 0)
                dst[i, :, lo:lo + w] = rows.astype(BF16)
        return store

    def to_twelfths(dst):
        def store(h, idx, c, w, value):
            lo = D // 2 * h + c
            for i in range(4):
                dst[i, :, lo:lo + w] = jnp.concatenate([value[12 * i:12 * i + 12], jnp.zeros((4, w), F32)], 0)
        return store

    def to_out(dst):
        def store(h, idx, c, w, value):
            dst[:, D // 2 * h + c:D // 2 * h + c + w] = value
        return store

    def all_to_all(g, src, dst):
        copies = []
        for by in (1, 2, 3):
            copies.append(pltpu.make_async_remote_copy(
                src_ref=src.at[peers[g][by]], dst_ref=dst.at[ranks[g]], send_sem=asend.at[g, by],
                recv_sem=arecv.at[g, ranks[g]], device_id={"dp": places[g][by]}, device_id_type=MESH))
        for c in copies:
            c.start()
        dst[ranks[g]] = src[ranks[g]]
        return copies

    def all_arrived(g, dst):
        for by in (1, 2, 3):
            there = dst.at[peers[g][by]]
            pltpu.make_async_remote_copy(
                src_ref=there, dst_ref=there, send_sem=asend.at[g, 0], recv_sem=arecv.at[g, peers[g][by]],
                device_id={"dp": places[g][1]}, device_id_type=MESH).wait_recv()

    swap_next()
    for one, store, following in ((d2, to_rows(d3s), d3), (u2, to_rows(u3s), u3), (q2, to_groups(q3s), q3)):
        one.middle()
        swap_next()
        one.finish(store)
        following.start(*everything)
    swap_next()
    for one in (u3, q3, d3):
        one.middle()
    u3.finish(to_twelfths(u4s))
    sent = all_to_all(U, u4s, u4r)
    q3.finish(to_twelfths(q4s))
    sent += all_to_all(Q, q4s, q4r)
    swap_next()
    sums[...] = vec[6]
    other = partner_copy(vec.at[6], sums_other, vsem)
    other.start()
    d3.finish(to_out(d_out))
    all_arrived(U, u4r)
    for i in range(4):
        u_out[:, i * D:(i + 1) * D] = u4r[i, 0:12, :]
    all_arrived(Q, q4r)
    for i in range(3):
        q_out[:, i * D:(i + 1) * D] = q4r[i, 0:12, :]
    o_out[...] = q4r[3, 0:12, :]

    present.wait()
    other.wait()
    for one in (d2, u2, q2, d3, u3, q3):
        one.drain()
    for copy in swaps + sent:
        copy.wait_send()
    for key, copy in remote.items():
        if key[2] == 0:
            copy.wait_send()

    @pl.when(sec == 1)
    def _():
        hand.wait_send()


def main(*args):
    vmem = pl.BlockSpec(memory_space=VM)
    hbm = pl.BlockSpec(memory_space=pltpu.HBM)
    dma = pltpu.SemaphoreType.DMA

    def half(*shape):
        return [VM((2, 2) + shape, BF16), VM((2,) + shape, BF16)]
    return pl.pallas_call(
        main_kernel,
        out_shape=[jax.ShapeDtypeStruct(dims, dtype) for dims, dtype in (
            ((2, 32, D), BF16), ((2, 32, D), BF16), ((12, 3 * D), F32), ((12, D), F32), ((12, FF), F32), ((48, D), F32),
            ((16, D), F32), ((16, D), F32), ((3, SLOTS, 4, R, D), BF16), ((3, SLOTS, 4, R, D), BF16))],
        in_specs=[vmem, vmem, pl.BlockSpec(memory_space=pltpu.SMEM), vmem] + [hbm] * 4 + [vmem] * 3,
        out_specs=[vmem] * 8 + [hbm] * 2,
        scratch_shapes=[
            VM((D, 3 * D), BF16), VM((D, D), BF16), VM((D, FF), BF16), VM((FF, D), BF16),
            VM((SLOTS, R, D), BF16), VM((2, 256, D), BF16), VM((2, 256, D), BF16), VM((SLOTS, 6, 256, 256), F32),
            VM((SLOTS, R, D), F32), VM((SLOTS, R, 128), F32), VM((SLOTS, R, D), F32), VM((SLOTS, R, 128), F32),
            VM((SLOTS, R, FF), F32), VM((R, D), BF16), VM((2, 256, D), F32), VM((2, 256, D), F32), VM((R, D), F32),
            VM((2, ROWS, D), BF16), VM((ROWS, D), BF16), VM((ROWS, FF), BF16), VM((ROWS, 4 * D), BF16),
            VM((ROWS, FF), BF16), VM((ROWS, D), BF16), VM((16, D), F32),
            VM((2, 32, D), BF16), VM((2, 2, 32, D), BF16), VM((R, D), BF16), VM((R, D), BF16), VM((2, 32, D), BF16),
            VM((4, 192, D), BF16), VM((4, 4, 48, D), BF16), VM((4, 4, 48, D), BF16),
            VM((4, 48, D), BF16), VM((4, 48, D), BF16), VM((4, 48, D), BF16)]
        + half(192, D // 2) + half(2, 48, D) + half(2, 48, D)
        + half(48, D // 2) + half(48, D // 2) + half(48, D // 2)
        + [VM((4, 16, D), F32)] * 4 + [VM((7, 16, D), F32), VM((6, 16, D), F32)]
        + [dma((4,)), dma((2,)), dma((2,)), dma((2,)), dma((3, 2)), dma((2,)),
           dma((2, 3, SLOTS, 4)), dma((2, 3, SLOTS, 4)), dma((2, 3)), dma((2, 3, 4)),
           dma((36,)), dma((36,)), dma((2, 4)), dma((2, 4)), dma((6,)), dma((6,))],
        compiler_params=pltpu.CompilerParams(collective_id=0, has_side_effects=True, vmem_limit_bytes=63 * 2**20),
        name="layers",
    )(*args)


def finish_kernel(keep, got, q_in, o_in, u_in, d_in, sums, other,
                  hidden, token, q_out, o_out, u_out, d_out, g_gains, g_bias, g_up, g_embed):
    sec = lax.axis_index("section")
    dp = lax.axis_index("dp")
    hidden[...] = jnp.where(sec == 0, got[...], keep[...])
    token[...] = jnp.where(sec == 0, keep[...], got[...])
    q_out[0] = q_in[...]
    o_out[0] = o_in[...]
    u_out[0] = u_in[...]
    d_out[0] = d_in[...]
    turned = pltpu.roll(sums[...], lax.rem(D - dp * 12, D), 1)
    g_gains[0] = turned[0:2, 0:12]
    g_bias[0] = turned[2:8, 0:12]
    lines = sums[12:13, :]
    for i in range(1, 4):
        lines = jnp.where(lax.div(dp, 16) == i, sums[12 + i:13 + i, :], lines)
    g_up[...] = pltpu.roll(lines, lax.rem(D - lax.rem(dp, 16) * 48, D), 1)[:, 0:48]
    mine, theirs = sums[8:12, :], other[8:12, :]
    rows = jnp.concatenate([jnp.where(sec == 0, mine, theirs)[0:1], jnp.where(sec == 0, theirs, mine)], 0)
    g_embed[...] = pltpu.roll(rows, lax.rem(D - (sec * 64 + dp) * 6, D), 1)[:, 0:6]


def finish(*args):
    vmem = pl.BlockSpec(memory_space=VM)
    return pl.pallas_call(
        finish_kernel,
        out_shape=[jax.ShapeDtypeStruct(dims, dtype) for dims, dtype in (
            ((2, 32, D), BF16), ((2, 32, D), BF16), ((1, 12, 3 * D), F32), ((1, 12, D), F32), ((1, 12, FF), F32),
            ((1, 48, D), F32), ((1, 2, 12), F32), ((1, 6, 12), F32), ((1, 48), F32), ((5, 6), F32))],
        in_specs=[vmem] * 8, out_specs=[vmem] * 10,
        name="finish",
    )(*args)


def local(*args):
    return tuple(finish(*main(*args)[:8]))


def solution(mesh):
    split = ("section",)
    placed = (
        P("dp", "section", None), P("dp", "section", None), P("dp"), P(),
        P("section", None, None), P("section", None, None), P("section", None, None), P("section", None, None),
        P("section", None, None), P("section", None, None), P("section", None))
    return jax.shard_map(
        local, mesh=mesh, in_specs=placed,
        out_specs=(
            P("dp", "section", None), P("dp", "section", None),
            P("section", "dp", None), P("section", "dp", None), P("section", "dp", None), P("section", "dp", None),
            P("section", None, "dp"), P("section", None, "dp"), P("section", "dp"), P(None, ("section", "dp"))),
        check_vma=False)
```

```python
import jax
import jax.numpy as jnp
import numpy as np
from jax import lax
from jax.experimental import pallas as pl
from jax.experimental.pallas import tpu as pltpu
from jax.sharding import PartitionSpec as P

F32 = jnp.float32
BF16 = jnp.bfloat16
VM = pltpu.VMEM
MESH = pl.DeviceIdType.MESH
D = 768
FF = 3072
SEQ = 64
R = 2 * SEQ
SLOTS = 4
ROWS = SLOTS * R
STEP = 256
KEYS = SLOTS * SEQ
STRIDE = {"y": 16, "x": 4, "z": 1}
Q, U, W = 0, 1, 2
AXES = ("x", "z", "y")


class Names:
    def __init__(self, **entries):
        self.__dict__.update(entries)


def nn(a, b):
    return jnp.dot(a, b, preferred_element_type=F32)


def nt(a, b):
    return lax.dot_general(a, b, (((1,), (1,)), ((), ())), preferred_element_type=F32)


def tn(a, b):
    return lax.dot_general(a, b, (((0,), (0,)), ((), ())), preferred_element_type=F32)


def lane_masks(value, dtype):
    lane = lax.broadcasted_iota(jnp.int32, (1, STEP), 1) // 64
    return [jnp.where(lane == h, value, 0.0).astype(dtype) for h in range(4)]


def norm_forward(u, gain, shift, hat_ref, inv_ref):
    out = []
    for r in range(0, R, 32):
        v = u[r:r + 32]
        centre = v - jnp.sum(v, -1, keepdims=True) * (1.0 / D)
        inv = lax.rsqrt(jnp.sum(centre * centre, -1, keepdims=True) * (1.0 / D) + 1e-5)
        hat = centre * inv
        hat_ref[r:r + 32] = hat
        inv_ref[r:r + 32] = jnp.broadcast_to(inv, (32, 128))
        out.append((hat * gain + shift).astype(BF16))
    return jnp.concatenate(out, 0)


def norm_backward(dy, gain, hat_ref, inv_ref):
    out, dgain, dshift = [], 0.0, 0.0
    for r in range(0, R, 32):
        g = dy[r:r + 32]
        hat = hat_ref[r:r + 32]
        inv = inv_ref[r:r + 32][:, :1]
        dgain = dgain + jnp.sum(g * hat, 0, keepdims=True)
        dshift = dshift + jnp.sum(g, 0, keepdims=True)
        gg = g * gain
        m1 = jnp.sum(gg, -1, keepdims=True) * (1.0 / D)
        m2 = jnp.sum(gg * hat, -1, keepdims=True) * (1.0 / D)
        out.append((gg - m1 - hat * m2) * inv)
    return jnp.concatenate(out, 0), dgain, dshift


def forward(j, u, w, p, s):
    rows = pl.ds(pl.multiple_of(j * R, R), R)
    slot = pl.ds(pl.multiple_of(j * SEQ, SEQ), SEQ)
    a = norm_forward(u, p.gain(0), p.bias(0), s.hat1.at[j], s.inv1.at[j])
    s.ao[0, rows] = a
    for n in range(0, 3 * D, STEP):
        k = n % D
        if k == 0:
            w.wait(j, n // D)
        c = nn(a, w.qkv[n // D, :, k:k + STEP])
        if n < D:
            s.dcz[rows, k:k + STEP] = (c + p.bias(1)[:, k:k + STEP]).astype(BF16)
        elif n < 2 * D:
            c = c.astype(BF16)
            for q in range(2):
                s.k[q, slot, k:k + STEP] = c[q * SEQ:(q + 1) * SEQ]
        else:
            c = (c + p.bias(2)[:, k:k + STEP]).astype(BF16)
            for q in range(2):
                s.v[q, slot, k:k + STEP] = c[q * SEQ:(q + 1) * SEQ]
    w.done(j, 0)
    ones = lane_masks(1.0, F32)
    eighth = lane_masks(0.125, BF16)
    col = lax.broadcasted_iota(jnp.int32, (SEQ, KEYS), 1)
    row = lax.broadcasted_iota(jnp.int32, (SEQ, KEYS), 0)
    allow = ((col & 63) <= row) & (col < (j + 1) * SEQ)
    veto = jnp.where(allow, 0.0, -1e30)
    veto = jnp.concatenate([veto] * 4, 0)
    for q in range(2):
        qrows = pl.ds(pl.multiple_of(j * R + q * SEQ, SEQ), SEQ)
        for g in range(3):
            cols = slice(g * STEP, (g + 1) * STEP)
            q4 = s.dcz[qrows, cols]
            q4 = jnp.concatenate([q4 * m for m in eighth], 0)
            sc = nt(q4, s.k[q, :, cols]) + veto
            ex = jnp.exp(sc - jnp.max(sc, -1, keepdims=True))
            pr = ex * (1.0 / jnp.sum(ex, -1, keepdims=True))
            s.p[j, 3 * q + g] = pr
            o4 = nn(pr.astype(BF16), s.v[q, :, cols])
            o = sum(o4[h * SEQ:(h + 1) * SEQ] * ones[h] for h in range(4))
            s.ao[1, qrows, cols] = o.astype(BF16)
    s.post(0, Q, j)
    o = s.ao[1, rows]
    w.wait(j, 3)
    m1 = u + (jnp.concatenate([nn(o, w.out[:, n:n + STEP]) for n in range(0, D, STEP)], 1) + p.bias(3))
    w.done(j, 1)
    b = norm_forward(m1, p.gain(1), p.bias(4), s.hat2.at[j], s.inv2.at[j])
    s.b[rows] = b
    s.post(0, U, j)
    w.wait(j, 4)
    for n in range(0, FF, STEP):
        f = nn(b, w.up[:, n:n + STEP]) + p.up(n, n + STEP)
        ff = f * f
        half = 0.5 + 0.5 * jnp.tanh(f * (0.7978845608 + (0.7978845608 * 0.044715) * ff))
        e = f * half
        s.e[rows, n:n + STEP] = e.astype(BF16)
        s.slope[j, :, n:n + STEP] = half + e * (1.0 - half) * (
            2 * 0.7978845608 + (6 * 0.7978845608 * 0.044715) * ff)
    w.done(j, 2)
    s.post(0, W, j)
    e = s.e[rows]
    w.wait(j, 5)
    r = jnp.concatenate([nn(e, w.down[:, n:n + STEP]) for n in range(0, D, STEP)], 1)
    w.done(j, 3)
    return m1 + (r + p.bias(5))


def backward(j, dr, w, p, s, t):
    rows = pl.ds(pl.multiple_of(j * R, R), R)
    slot = pl.ds(pl.multiple_of(j * SEQ, SEQ), SEQ)
    dr2 = dr.astype(BF16)
    s.dr[rows] = dr2
    s.post(1, W, j)
    t.add(2 + 5, jnp.sum(dr, 0, keepdims=True))
    w.ready(j, 2)
    for n in range(0, FF, STEP):
        de = nn(dr2, w.up[:, n:n + STEP])
        df = s.slope[j, :, n:n + STEP] * de
        t.add(12 + n // D, jnp.sum(df, 0, keepdims=True), n % D)
        s.df[rows, n:n + STEP] = df.astype(BF16)
    s.post(1, U, j)
    df = s.df[rows]
    w.ready(j, 3)
    db = jnp.concatenate([nn(df, w.down[:, n:n + STEP]) for n in range(0, D, STEP)], 1)
    dm, dgain, dshift = norm_backward(db, p.gain(1), s.hat2.at[j], s.inv2.at[j])
    t.add(1, dgain)
    t.add(2 + 4, dshift)
    dm1 = dr + dm
    dz = dm1.astype(BF16)
    s.dcz[rows, 3 * D:] = dz
    t.add(2 + 3, jnp.sum(dm1, 0, keepdims=True))
    w.ready(j, 1)
    for n in range(0, D, STEP):
        s.dcz[rows, 2 * D + n:2 * D + n + STEP] = nn(dz, w.out[:, n:n + STEP]).astype(BF16)
    ones = lane_masks(1.0, BF16)
    eighth = lane_masks(0.125, BF16)
    eighth32 = lane_masks(0.125, F32)
    for q in range(2):
        drows = pl.ds(pl.multiple_of(j * R + q * SEQ, SEQ), SEQ)
        for g in range(3):
            cols = slice(g * STEP, (g + 1) * STEP)
            do4 = s.dcz[drows, 2 * D + g * STEP:2 * D + (g + 1) * STEP]
            do4 = jnp.concatenate([do4 * m for m in ones], 0)
            q4 = s.dcz[drows, cols]
            q4 = jnp.concatenate([q4 * m for m in eighth], 0)
            dp = nt(do4, s.v[q, :, cols])
            pr = s.p[j, 3 * q + g]
            ds = (pr * (dp - jnp.sum(pr * dp, -1, keepdims=True))).astype(BF16)
            dq4 = nn(ds, s.k[q, :, cols])
            dq = sum(dq4[h * SEQ:(h + 1) * SEQ] * eighth32[h] for h in range(4))
            t.add(2 + 1, jnp.sum(dq, 0, keepdims=True), g * STEP)
            s.dcz[drows, cols] = dq.astype(BF16)
            s.dk[q, :, cols] = s.dk[q, :, cols] + tn(ds, q4)
            s.dv[q, :, cols] = s.dv[q, :, cols] + tn(pr.astype(BF16), do4)
            s.dcz[drows, D + g * STEP:D + (g + 1) * STEP] = s.dk[q, slot, cols].astype(BF16)
            dv = s.dv[q, slot, cols]
            s.dcz[drows, 2 * D + g * STEP:2 * D + (g + 1) * STEP] = dv.astype(BF16)
            t.add(2 + 2, jnp.sum(dv, 0, keepdims=True), g * STEP)
    s.post(1, Q, j)
    dc = s.dcz[rows, 0:3 * D]
    w.ready(j, 0)
    back = w.qkv.reshape(3 * D, D)
    da = jnp.concatenate([nn(dc, back[:, n:n + STEP]) for n in range(0, D, STEP)], 1)
    dx, dgain, dshift = norm_backward(da, p.gain(0), s.hat1.at[j], s.inv1.at[j])
    t.add(0, dgain)
    t.add(2, dshift)
    return dm1 + dx


def partner_copy(src, dst, sems):
    return pltpu.make_async_remote_copy(
        src_ref=src, dst_ref=dst, send_sem=sems.at[0], recv_sem=sems.at[1],
        device_id={"section": 1 - lax.axis_index("section")}, device_id_type=MESH)


def rank(axis):
    return lax.rem(lax.div(lax.axis_index("dp"), STRIDE[axis]), 4)


def main_kernel(tokens, out_grad, passes, embed, w_qkv, w_out, w_up, w_down, gains, biases, up_bias,
                keep, got, q_out, o_out, u_out, d_out, sums, sums_other, xs, turned,
                qkv_v, out_v, up_v, down_v, k, v, prob, hat1, inv1, hat2, inv2, slope, dk, dv, state,
                ao, b, e, dcz, df, dr, small, halves, leave, arrive, give, y0, entry,
                q2s, u2s, d2s, d3s, q2r, u2r, d2r, d3r,
                q4s, u4s, q4r, u4r, vec, vec_in,
                wsem, tsem, usem, xsem, hsem, gsem, psem, vsem, psend, precv, plocal, stage, esend, erecv,
                asend, arecv, ssend, srecv):
    sec = lax.axis_index("section")
    dp = lax.axis_index("dp")
    loads = [pltpu.make_async_copy(w_qkv.at[0, :, pl.ds(i * D, D)], qkv_v.at[i], wsem.at[i]) for i in range(3)]
    loads += [pltpu.make_async_copy(src.at[0], dst, wsem.at[3 + i]) for i, (src, dst) in enumerate(
        ((w_out, out_v), (w_up, up_v), (w_down, down_v)))]
    for c in loads:
        c.start()
    ranks = [rank(axis) for axis in AXES]
    peers = [[lax.rem(ranks[g] + by, 4) for by in range(4)] for g in range(3)]
    places = [[dp + (peers[g][by] - ranks[g]) * STRIDE[AXES[g]] for by in range(4)] for g in range(3)]
    offsets = [[pl.multiple_of(peers[g][by] * D, D) for by in range(4)] for g in range(3)]
    seconds = [lax.div(peers[Q][by], 3) for by in range(4)]
    barrier = pltpu.get_barrier_semaphore()
    for g in range(3):
        for by in (1, 2, 3):
            pl.semaphore_signal(barrier, inc=1, device_id={"dp": places[g][by]}, device_id_type=MESH)
            pl.semaphore_signal(barrier, inc=1, device_id={"dp": places[g][by], "section": 1 - sec},
                                device_id_type=MESH)
    planes = {}
    for g, axis in ((U, "y"), (Q, "z")):
        pos = rank(axis)
        planes[g] = [[places[g][by] + (lax.rem(pos + over, 4) - pos) * STRIDE[axis] for by in range(4)]
                     for over in range(4)]
        for over in (1, 2, 3):
            for by in (1, 2, 3):
                pl.semaphore_signal(barrier, inc=1, device_id={"dp": planes[g][over][by]}, device_id_type=MESH)
    pl.semaphore_signal(barrier, inc=1, device_id={"section": 1 - sec}, device_id_type=MESH)
    give[...] = jnp.where(sec == 0, out_grad[...], tokens[...])
    own = jnp.where(sec == 0, tokens[...], out_grad[...])
    pl.semaphore_wait(barrier, 37)
    exchange = partner_copy(give, halves.at[sec], xsem)
    exchange.start()
    halves[sec] = own

    wide = (dcz, df, e)

    def source(which, g, j, by):
        rows = pl.ds(pl.multiple_of(j * R, R), R)
        if g == Q:
            return ao.at[seconds[by], rows] if which == 0 else dcz.at[rows, pl.ds(offsets[g][by], D)]
        if g == U:
            return b.at[rows] if which == 0 else df.at[rows, pl.ds(offsets[g][by], D)]
        return e.at[rows, pl.ds(offsets[g][by], D)] if which == 0 else dr.at[rows]

    def target(which, g, j, by, first):
        if which == 0:
            return xs.at[g, j, peers[g][by]]
        if first:
            return y0.at[g, peers[g][by]]
        return wide[g].at[pl.ds(pl.multiple_of(j * R, R), R), pl.ds(offsets[g][by], D)]

    def remote(which, g, j, by, first):
        return pltpu.make_async_remote_copy(
            src_ref=source(which, g, j, by), dst_ref=target(which, g, j, 0, first),
            send_sem=psend.at[which, g, j, by], recv_sem=precv.at[which, g, j, ranks[g]],
            device_id={"dp": places[g][by], "section": sec if first else 1 - sec}, device_id_type=MESH)

    def inside(which, g):
        return pltpu.make_async_copy(source(which, g, 0, 0), target(which, g, 0, 0, True), plocal.at[which, g])

    def post(which, g, j):
        @pl.when(j == 0)
        def _():
            for by in (2, 1, 3):
                remote(which, g, 0, by, True).start()
            inside(which, g).start()

        @pl.when(j > 0)
        def _():
            for by in (2, 1, 3, 0):
                remote(which, g, j, by, False).start()

    def arrived(which, g, j, first=False):
        for by in range(1 if first else 0, 4):
            there = target(which, g, j, by, first)
            pltpu.make_async_remote_copy(
                src_ref=there, dst_ref=there, send_sem=psend.at[which, g, 0, 0],
                recv_sem=precv.at[which, g, j, peers[g][by]],
                device_id={"dp": places[g][1]}, device_id_type=MESH).wait_recv()
        if first:
            inside(which, g).wait()

    class Sum:
        def __init__(self, g, m, n):
            if g == Q:
                self.refs = [r.at[1 + m, :, pl.ds(n * STEP, STEP)] for r in (hat1, hat2)]
            else:
                at = 2 * (n + (3 if g == U else 0))
                self.refs = [slope.at[1 + m, :, pl.ds((at + h) * STEP, STEP)] for h in range(2)]

        def read(self):
            return jnp.concatenate([r[...] for r in self.refs], 0)

        def write(self, value):
            size = STEP // len(self.refs)
            for i, r in enumerate(self.refs):
                r[...] = value[i * size:(i + 1) * size]

    tiles = [(m, n) for m in range(3) for n in range(3)]
    stacks = {Q: q2s, U: u2s, W: d2s}
    second = {g: r.reshape(D, D) for g, r in stacks.items()}

    def turn(first):
        blocks = [(qkv_v.at[i], 0) for i in range(3)] + [(out_v, 0)]
        blocks += [(down_v.at[pl.ds(i * D, D)], 0) for i in range(4)] + [(up_v, i * D) for i in range(4)]
        copies = []
        for i, (src, lo) in enumerate(blocks):
            if first:
                for order in {0: (0,), 1: (1,), 2: (2,), 3: (3,), 4: (5,), 8: (4,)}.get(i, ()):
                    loads[order].wait()
            if i >= 3:
                copies[i - 3].wait()
            dst = second[i % 3]
            def flip(m, carry):
                at = pl.multiple_of(m * STEP, STEP)
                for n in range(3):
                    dst[n * STEP:(n + 1) * STEP, pl.ds(at, STEP)] = src[
                        pl.ds(at, STEP), lo + n * STEP:lo + (n + 1) * STEP].T
                return carry
            lax.fori_loop(0, 3, flip, 0)
            copies.append(pltpu.make_async_copy(dst, turned.at[i], tsem.at[i]))
            copies[-1].start()
        for c in copies[-3:]:
            c.wait()

    returns = [[pltpu.make_async_copy(turned.at[pl.ds(0, 3)], qkv_v, usem.at[0])],
               [pltpu.make_async_copy(turned.at[3], out_v, usem.at[1])],
               [pltpu.make_async_copy(turned.at[4 + i], up_v.at[:, pl.ds(i * D, D)], usem.at[2 + i])
                for i in range(4)],
               [pltpu.make_async_copy(turned.at[8 + i], down_v.at[pl.ds(i * D, D)], usem.at[6 + i])
                for i in range(4)]]

    w = Names(qkv=qkv_v, out=out_v, up=up_v, down=down_v)

    def wait(j, i):
        @pl.when((j == 0) & (sec == 0))
        def _():
            loads[i].wait()

    def done(j, i):
        @pl.when(j == SLOTS - 1)
        def _():
            for c in returns[i]:
                c.start()

    def ready(j, i):
        @pl.when(j == SLOTS - 1)
        def _():
            for c in returns[i]:
                c.wait()
    w.wait, w.done, w.ready = wait, done, ready
    p = Names(gain=lambda i: gains[0, i:i + 1, :], bias=lambda i: biases[i],
              up=lambda lo, hi: up_bias[:, lo:hi])
    s = Names(k=k, v=v, p=prob, hat1=hat1, inv1=inv1, hat2=hat2, inv2=inv2, slope=slope, dk=dk, dv=dv,
              ao=ao, b=b, e=e, dcz=dcz, df=df, dr=dr, post=post)
    small[...] = jnp.zeros_like(small)

    def add(i, value, at=0):
        cols = slice(at, at + value.shape[1])
        small[i:i + 1, cols] = small[i:i + 1, cols] + value
    t = Names(add=add)
    k[...] = jnp.zeros_like(k)
    v[...] = jnp.zeros_like(v)
    dk[...] = jnp.zeros_like(dk)
    dv[...] = jnp.zeros_like(dv)
    row = lax.broadcasted_iota(jnp.int32, (R, 1), 0)
    count = jnp.where(row < SEQ, passes[0], passes[1]) - 1
    count = jnp.where(sec == 0, SLOTS, count)
    hand = partner_copy(leave, arrive, hsem)
    present = partner_copy(give, got, gsem)
    partial = [partner_copy(r, r, psem.at[i]) for i, r in enumerate((q2s, u2s, d2s))]

    def joined():
        return jnp.concatenate([halves[h, i] for i in range(2) for h in range(2)], 0).astype(F32)

    slots = jnp.where(sec == 0, 1, SLOTS)

    def step_forward(j, carry):
        h = state[...]
        r = forward(j, h + embed[pl.ds(j + sec, 1), :], w, p, s)
        state[...] = jnp.where(count > j, r, h)
        return carry

    def step_backward(i, carry):
        j = slots - 1 - i
        g = state[...]
        du = backward(j, jnp.where(count > j, g, 0.0), w, p, s, t)
        entry[j] = jnp.sum(du, 0, keepdims=True)
        state[...] = jnp.where(count > j, du, g)
        return carry

    @pl.when(sec == 0)
    def _():
        exchange.wait()
        state[...] = joined()

    @pl.when(sec == 1)
    def _():
        turn(True)
        exchange.wait()
        hand.wait_recv()
        state[...] = arrive[...].astype(F32)

    lax.fori_loop(0, slots, step_forward, 0)

    @pl.when(sec == 0)
    def _():
        leave[...] = state[...].astype(BF16)
        hand.start()
        turn(False)
        for group in returns:
            for c in group:
                c.start()

        def staging(g, j):
            return [pltpu.make_async_copy(xs.at[g, j, i], second[g].at[pl.ds(i * R, R)], stage.at[g, i])
                    for i in range(4)]

        def bring(g, j):
            arrived(0, g, j)
            for c in staging(g, j):
                c.start()

        def clear(m, carry):
            for g in range(3):
                for n in range(3):
                    Sum(g, m, n).write(jnp.zeros((STEP, STEP), F32))
            return carry
        lax.fori_loop(0, 3, clear, 0)
        for g in (W, U, Q):
            bring(g, SLOTS - 1)
        for group in returns:
            for c in group:
                c.wait()

        def gather(i, carry):
            j = SLOTS - 1 - i
            rows = pl.ds(pl.multiple_of(j * R, R), R)
            for g in (W, U, Q):
                for c in staging(g, j):
                    c.wait()
                arrived(1, g, j)

                def across(m, carry):
                    left = second[g][0:ROWS, pl.ds(pl.multiple_of(m * STEP, STEP), STEP)]
                    for n in range(3):
                        right = jnp.concatenate([
                            wide[g][rows, x * D + n * STEP:x * D + (n + 1) * STEP] for x in range(4)], 0)
                        held = Sum(g, m, n)
                        held.write(held.read() + tn(left, right))
                    return carry
                lax.fori_loop(0, 3, across, 0)

                @pl.when(j > 1)
                def _():
                    bring(g, j - 1)

                @pl.when(j == 1)
                def _():
                    def rounded(m, carry):
                        there = pl.ds(pl.multiple_of(m * STEP, STEP), STEP)
                        for n in range(3):
                            second[g][there, n * STEP:(n + 1) * STEP] = Sum(g, m, n).read().astype(BF16)
                        return carry
                    lax.fori_loop(0, 3, rounded, 0)
                    partial[g].start()
            return carry
        lax.fori_loop(0, SLOTS - 1, gather, 0)
        hand.wait()
        state[...] = arrive[...].astype(F32)

    @pl.when(sec == 1)
    def _():
        final = state[...].astype(BF16)
        for i in range(2):
            give[i] = final[i * SEQ:i * SEQ + 32]
            keep[i] = final[i * SEQ + 32:i * SEQ + 64]
        present.start()
        state[...] = joined()

    lax.fori_loop(0, slots, step_backward, 0)
    fetched = [[pltpu.make_async_copy(xs.at[g, 0, i], up_v.at[pl.ds(i * R, R), pl.ds(g * D, D)], stage.at[g, i])
                for i in range(4)] for g in range(3)]
    for g in (W, U, Q):
        arrived(0, g, 0, True)
        for c in fetched[g]:
            c.start()

    @pl.when(sec == 0)
    def _():
        final = state[...].astype(BF16)
        for i in range(2):
            keep[i] = final[i * SEQ:i * SEQ + 32]
            give[i] = final[i * SEQ + 32:i * SEQ + 64]
        present.start()
        for g in range(3):
            partial[g].wait_send()

    @pl.when(sec == 1)
    def _():
        leave[...] = state[...].astype(BF16)
        hand.start()

    def shares(axis, number):
        pos = rank(axis)
        copies = []
        for by in (1, 2, 3):
            there = dp + (lax.rem(pos + by, 4) - pos) * STRIDE[axis]
            copies.append(pltpu.make_async_remote_copy(
                src_ref=vec.at[number], dst_ref=vec_in.at[number, by - 1], send_sem=ssend.at[number, by - 1],
                recv_sem=srecv.at[number, by - 1], device_id={"dp": there}, device_id_type=MESH))
        return copies
    shared = [shares(axis, number) for number, axis in enumerate(("z", "y", "x"))]

    def share_start(number):
        for c in shared[number]:
            c.start()

    def share_next(number):
        for c in shared[number]:
            c.wait_recv()
        vec[number + 1] = vec[number] + vec_in[number, 0] + vec_in[number, 1] + vec_in[number, 2]
        if number < 2:
            share_start(number + 1)
    vec[0] = small[...]
    for j in range(SLOTS):
        vec[0, 8 + j:9 + j, :] = entry[j]
    share_start(0)

    class Part:
        def __init__(self, axis, number, block, landing):
            self.axis, self.number, self.block, self.landing = axis, number, block, landing
            self.pos = rank(axis)

        def copies(self, c):
            made = []
            for by in (2, 1, 3):
                to = lax.rem(self.pos + by, 4)
                made.append(pltpu.make_async_remote_copy(
                    src_ref=self.block(to, columns(c)), dst_ref=self.landing(by - 1, columns(c)),
                    send_sem=esend.at[self.number, c, by - 1], recv_sem=erecv.at[self.number, c, by - 1],
                    device_id={"dp": dp + (to - self.pos) * STRIDE[self.axis]}, device_id_type=MESH))
            return made

        def start(self, c):
            for copy in self.copies(c):
                copy.start()

        def finish(self, c, store):
            for copy in self.copies(c):
                copy.wait_recv()
            own = self.block(self.pos, columns(c))
            others = [self.landing(i, columns(c)) for i in range(3)]
            for i in range(4 if len(own.shape) == 3 else 1):
                key = (i,) if len(own.shape) == 3 else (slice(None),)
                value = own[key].astype(F32)
                for other in others:
                    value = value + other[key].astype(F32)
                store(i, columns(c), value)

        def drain(self, c):
            for copy in self.copies(c):
                copy.wait_send()

    def columns(c):
        return pl.ds(pl.multiple_of(c * STEP, STEP), STEP)

    d2 = Part("z", 0, lambda i, c: d2s.at[:, i, :, c], lambda i, c: d2r.at[i, :, :, c])
    u2 = Part("x", 1, lambda i, c: u2s.at[:, i, :, c], lambda i, c: u2r.at[i, :, :, c])
    q2 = Part("y", 2, lambda i, c: q2s.at[i, :, c], lambda i, c: q2r.at[i, :, c])
    d3 = Part("x", 3, lambda i, c: d3s.at[i, :, c], lambda i, c: d3r.at[i, :, c])

    def each(body):
        def step(c, carry):
            body(c)
            return carry
        lax.fori_loop(0, 3, step, 0)

    def multiply(g, one):
        for c in fetched[g]:
            c.wait()
        arrived(1, g, 0, True)

        @pl.when(sec == 1)
        def _():
            partial[g].wait_recv()

        def across(c):
            right = y0[g, :, :, columns(c)].reshape(ROWS, STEP)
            for m in range(3):
                part = second[g].at[m * STEP:(m + 1) * STEP, columns(c)]
                held = jnp.where(sec == 1, part[...].astype(F32), 0.0)
                left = up_v[0:ROWS, g * D + m * STEP:g * D + (m + 1) * STEP]
                part[...] = (held + tn(left, right)).astype(BF16)
            one.start(c)
        each(across)

    def to_rows(dst):
        def store(i, at, value):
            dst[i, :, at] = value.astype(BF16)
        return store

    def twelve(rows):
        return jnp.concatenate([rows, jnp.zeros((4, STEP), F32)], 0).astype(BF16)

    def to_plane_u(y, at, value):
        for z in range(4):
            u4s[y, z, :, at] = twelve(value[12 * z:12 * z + 12])

    def to_plane_q(i, at, value):
        for x in range(4):
            for z in range(4):
                q4s[z, x, :, at] = twelve(value[48 * x + 12 * z:48 * x + 12 * z + 12])

    def to_out(i, at, value):
        d_out[:, at] = value

    def plane(g, src, dst):
        axis = "y" if g == U else "z"
        pos = rank(axis)
        return [pltpu.make_async_remote_copy(
            src_ref=src.at[lax.rem(pos + over, 4), peers[g][by]], dst_ref=dst.at[over, ranks[g]],
            send_sem=asend.at[g, over, by], recv_sem=arecv.at[g, over, ranks[g]],
            device_id={"dp": planes[g][over][by]}, device_id_type=MESH)
            for over in range(4) for by in range(4) if over or by]

    def plane_sum(g, dst, r):
        value = dst[0, r].astype(F32)
        for over in (1, 2, 3):
            value = value + dst[over, r].astype(F32)
        return value[0:12]

    def plane_arrived(g, dst):
        for over in range(4):
            for by in range(4):
                if over or by:
                    there = dst.at[over, peers[g][by]]
                    pltpu.make_async_remote_copy(
                        src_ref=there, dst_ref=there, send_sem=asend.at[g, 0, 0],
                        recv_sem=arecv.at[g, over, peers[g][by]],
                        device_id={"dp": places[g][1]}, device_id_type=MESH).wait_recv()

    multiply(W, d2)
    multiply(U, u2)
    multiply(Q, q2)
    share_next(0)

    for which in range(2):
        for g in range(3):
            for by in (1, 2, 3):
                remote(which, g, 0, by, True).wait_send()

    @pl.when(sec == 1)
    def _():
        hand.wait_send()

        def drain(j, carry):
            for which in range(2):
                for g in range(3):
                    for by in range(4):
                        remote(which, g, j, by, False).wait_send()
            return carry
        lax.fori_loop(1, SLOTS, drain, 0)
    present.wait()

    def second_done(c):
        u2.finish(c, to_plane_u)
        d2.finish(c, to_rows(d3s))
        d3.start(c)
    each(second_done)
    spread_u = plane(U, u4s, u4r)
    for copy in spread_u:
        copy.start()
    u4r[0, ranks[U]] = u4s[rank("y"), ranks[U]]
    each(lambda c: q2.finish(c, to_plane_q))
    spread_q = plane(Q, q4s, q4r)
    for copy in spread_q:
        copy.start()
    q4r[0, ranks[Q]] = q4s[rank("z"), ranks[Q]]
    share_next(1)

    def drained(c):
        for one in (d2, u2, q2):
            one.drain(c)
    each(drained)
    each(lambda c: d3.finish(c, to_out))
    share_next(2)
    sums[...] = vec[3]
    other = partner_copy(vec.at[3], sums_other, vsem)
    other.start()
    plane_arrived(U, u4r)
    for i in range(4):
        u_out[:, i * D:(i + 1) * D] = plane_sum(U, u4r, i)
    plane_arrived(Q, q4r)
    for i in range(3):
        q_out[:, i * D:(i + 1) * D] = plane_sum(Q, q4r, i)
    o_out[...] = plane_sum(Q, q4r, 3)
    each(lambda c: d3.drain(c))
    for copies in shared + [spread_u, spread_q]:
        for copy in copies:
            copy.wait_send()
    other.wait()


def main(*args):
    vmem = pl.BlockSpec(memory_space=VM)
    hbm = pl.BlockSpec(memory_space=pltpu.HBM)
    dma = pltpu.SemaphoreType.DMA
    return pl.pallas_call(
        main_kernel,
        out_shape=[jax.ShapeDtypeStruct(dims, dtype) for dims, dtype in (
            ((2, 32, D), BF16), ((2, 32, D), BF16), ((12, 3 * D), F32), ((12, D), F32), ((12, FF), F32), ((48, D), F32),
            ((16, D), F32), ((16, D), F32), ((3, SLOTS, 4, R, D), BF16), ((12, D, D), BF16))],
        in_specs=[vmem, vmem, pl.BlockSpec(memory_space=pltpu.SMEM), vmem] + [hbm] * 4 + [vmem] * 3,
        out_specs=[vmem] * 8 + [hbm] * 2,
        scratch_shapes=[
            VM((3, D, D), BF16), VM((D, D), BF16), VM((D, FF), BF16), VM((FF, D), BF16),
            VM((2, 256, D), BF16), VM((2, 256, D), BF16), VM((SLOTS, 6, 256, 256), F32),
            VM((SLOTS, R, D), F32), VM((SLOTS, R, 128), F32), VM((SLOTS, R, D), F32), VM((SLOTS, R, 128), F32),
            VM((SLOTS, R, FF), F32), VM((2, 256, D), F32), VM((2, 256, D), F32), VM((R, D), F32),
            VM((2, ROWS, D), BF16), VM((ROWS, D), BF16), VM((ROWS, FF), BF16), VM((ROWS, 4 * D), BF16),
            VM((ROWS, FF), BF16), VM((ROWS, D), BF16), VM((16, D), F32),
            VM((2, 2, 32, D), BF16), VM((R, D), BF16), VM((R, D), BF16), VM((2, 32, D), BF16),
            VM((3, 4, R, D), BF16), VM((SLOTS, 1, D), F32),
            VM((4, 192, D), BF16), VM((4, 4, 48, D), BF16), VM((4, 4, 48, D), BF16),
            VM((4, 48, D), BF16),
            VM((3, 192, D), BF16), VM((3, 4, 48, D), BF16), VM((3, 4, 48, D), BF16),
            VM((3, 48, D), BF16)]
        + [VM((4, 4, 16, D), BF16)] * 4 + [VM((4, 16, D), F32), VM((3, 3, 16, D), F32)]
        + [dma((6,)), dma((12,)), dma((10,)), dma((2,)), dma((2,)), dma((2,)), dma((3, 2)), dma((2,)),
           dma((2, 3, SLOTS, 4)), dma((2, 3, SLOTS, 4)), dma((2, 3)), dma((3, 4)), dma((4, 3, 3)), dma((4, 3, 3)),
           dma((2, 4, 4)), dma((2, 4, 4)), dma((3, 3)), dma((3, 3))],
        compiler_params=pltpu.CompilerParams(collective_id=0, has_side_effects=True, vmem_limit_bytes=int(63.4 * 2**20)),
        name="layers",
    )(*args)


def finish_kernel(keep, got, q_in, o_in, u_in, d_in, sums, other,
                  hidden, token, q_out, o_out, u_out, d_out, g_gains, g_bias, g_up, g_embed):
    sec = lax.axis_index("section")
    dp = lax.axis_index("dp")
    hidden[...] = jnp.where(sec == 0, got[...], keep[...])
    token[...] = jnp.where(sec == 0, keep[...], got[...])
    for i in range(12):
        q_out[i] = q_in[i:i + 1, :]
        o_out[i] = o_in[i:i + 1, :]
        u_out[i] = u_in[i:i + 1, :]
    d_out[0] = d_in[...]
    turned = pltpu.roll(sums[...], lax.rem(D - dp * 12, D), 1)
    g_gains[0] = turned[0:2, 0:12]
    for i in range(6):
        g_bias[i] = turned[2 + i:3 + i, 0:12]
    lines = sums[12:13, :]
    for i in range(1, 4):
        lines = jnp.where(lax.div(dp, 16) == i, sums[12 + i:13 + i, :], lines)
    g_up[...] = pltpu.roll(lines, lax.rem(D - lax.rem(dp, 16) * 48, D), 1)[:, 0:48]
    mine, theirs = sums[8:12, :], other[8:12, :]
    rows = jnp.concatenate([jnp.where(sec == 0, mine, theirs)[0:1], jnp.where(sec == 0, theirs, mine)], 0)
    g_embed[...] = pltpu.roll(rows, lax.rem(D - (sec * 64 + dp) * 6, D), 1)[:, 0:6]


def finish(*args):
    vmem = pl.BlockSpec(memory_space=VM)
    return pl.pallas_call(
        finish_kernel,
        out_shape=[jax.ShapeDtypeStruct(dims, dtype) for dims, dtype in (
            ((2, 32, D), BF16), ((2, 32, D), BF16), ((12, 1, 3 * D), F32), ((12, 1, D), F32), ((12, 1, FF), F32),
            ((1, 48, D), F32), ((1, 2, 12), F32), ((6, 1, 12), F32), ((1, 48), F32), ((5, 6), F32))],
        in_specs=[vmem] * 8, out_specs=[vmem] * 10,
        name="finish",
    )(*args)


def local(*args):
    args = list(args)
    args[9] = jnp.swapaxes(args[9], 0, 1)
    outs = list(finish(*main(*args)[:8]))
    for i in (2, 3, 4, 7):
        outs[i] = jnp.swapaxes(outs[i], 0, 1)
    return tuple(outs)


def solution(mesh):
    split = ("section",)
    placed = (
        P("dp", "section", None), P("dp", "section", None), P("dp"), P(),
        P("section", None, None), P("section", None, None), P("section", None, None), P("section", None, None),
        P("section", None, None), P("section", None, None), P("section", None))
    return jax.shard_map(
        local, mesh=mesh, in_specs=placed,
        out_specs=(
            P("dp", "section", None), P("dp", "section", None),
            P("section", "dp", None), P("section", "dp", None), P("section", "dp", None), P("section", "dp", None),
            P("section", None, "dp"), P("section", None, "dp"), P("section", "dp"), P(None, ("section", "dp"))),
        check_vma=False)
```

```python
import jax
import jax.numpy as jnp
import numpy as np
from jax import lax
from jax.experimental import pallas as pl
from jax.experimental.pallas import tpu as pltpu
from jax.sharding import PartitionSpec as P

F32 = jnp.float32
BF16 = jnp.bfloat16
VM = pltpu.VMEM
MESH = pl.DeviceIdType.MESH
D = 768
FF = 3072
SEQ = 64
R = 2 * SEQ
SLOTS = 4
ROWS = SLOTS * R
STEP = 256
STRIDE = {"y": 16, "x": 4, "z": 1}
Q, U, W = 0, 1, 2
AXES = ("x", "z", "y")


class Names:
    def __init__(self, **entries):
        self.__dict__.update(entries)


def nn(a, b):
    return jnp.dot(a, b, preferred_element_type=F32)


def nt(a, b):
    return lax.dot_general(a, b, (((1,), (1,)), ((), ())), preferred_element_type=F32)


def tn(a, b):
    return lax.dot_general(a, b, (((0,), (0,)), ((), ())), preferred_element_type=F32)


def lane_masks(value, dtype):
    lane = lax.broadcasted_iota(jnp.int32, (1, STEP), 1) // 64
    return [jnp.where(lane == h, value, 0.0).astype(dtype) for h in range(4)]


def norm_forward(u, gain, shift, hat_ref, inv_ref):
    out = []
    for r in range(0, R, 32):
        v = u[r:r + 32]
        centre = v - jnp.sum(v, -1, keepdims=True) * (1.0 / D)
        inv = lax.rsqrt(jnp.sum(centre * centre, -1, keepdims=True) * (1.0 / D) + 1e-5)
        hat = centre * inv
        hat_ref[r:r + 32] = hat
        inv_ref[r:r + 32] = jnp.broadcast_to(inv, (32, 128))
        out.append((hat * gain + shift).astype(BF16))
    return jnp.concatenate(out, 0)


def norm_backward(dy, gain, hat_ref, inv_ref):
    out, dgain, dshift = [], 0.0, 0.0
    for r in range(0, R, 32):
        g = dy[r:r + 32]
        hat = hat_ref[r:r + 32]
        inv = inv_ref[r:r + 32][:, :1]
        dgain = dgain + jnp.sum(g * hat, 0, keepdims=True)
        dshift = dshift + jnp.sum(g, 0, keepdims=True)
        gg = g * gain
        m1 = jnp.sum(gg, -1, keepdims=True) * (1.0 / D)
        m2 = jnp.sum(gg * hat, -1, keepdims=True) * (1.0 / D)
        out.append((gg - m1 - hat * m2) * inv)
    return jnp.concatenate(out, 0), dgain, dshift


def keys_of(j):
    return 128 if j < 2 else 256


def p_at(s, j):
    return s.p.at[0, :, 128 * j:128 * (j + 1)] if j < 2 else s.p.at[j - 1]


def forward(j, u, w, p, s):
    rows = slice(j * R, (j + 1) * R)
    a = norm_forward(u, p.gain(0), p.bias(0), s.hat1.at[j], s.inv1.at[j])
    s.ao[0, rows] = a
    for n in range(0, 3 * D, STEP):
        k = n % D
        if k == 0:
            w.wait(j, n // D)
        c = nn(a, w.qkv[n // D, :, k:k + STEP])
        if n < D:
            s.dcz[rows, k:k + STEP] = (c + p.bias(1)[:, k:k + STEP]).astype(BF16)
        elif n < 2 * D:
            c = c.astype(BF16)
            for q in range(2):
                s.k[q, j * SEQ:(j + 1) * SEQ, k:k + STEP] = c[q * SEQ:(q + 1) * SEQ]
        else:
            c = (c + p.bias(2)[:, k:k + STEP]).astype(BF16)
            for q in range(2):
                s.v[q, j * SEQ:(j + 1) * SEQ, k:k + STEP] = c[q * SEQ:(q + 1) * SEQ]
    w.done(j, 0)
    nk = keys_of(j)
    ones = lane_masks(1.0, F32)
    eighth = lane_masks(0.125, BF16)
    key = lax.broadcasted_iota(jnp.int32, (nk, STEP), 0)
    place = lax.broadcasted_iota(jnp.int32, (nk, STEP), 1) & 63
    allow = ((key & 63) <= place) & (key < (j + 1) * SEQ)
    veto = jnp.where(allow, 0.0, -1e30)
    for q in range(2):
        qrows = slice(q * SEQ, (q + 1) * SEQ)
        for g in range(3):
            cols = slice(g * STEP, (g + 1) * STEP)
            q4 = s.dcz[j * R + q * SEQ:j * R + (q + 1) * SEQ, cols]
            q4 = jnp.concatenate([q4 * m for m in eighth], 0)
            sc = nt(s.k[q, 0:nk, cols], q4) + veto
            ex = jnp.exp(sc - jnp.max(sc, 0, keepdims=True))
            pr = ex * (1.0 / jnp.sum(ex, 0, keepdims=True))
            p_at(s, j)[3 * q + g] = pr
            o4 = tn(pr.astype(BF16), s.v[q, 0:nk, cols])
            o = sum(o4[h * SEQ:(h + 1) * SEQ] * ones[h] for h in range(4))
            s.ao[1, j * R + q * SEQ:j * R + (q + 1) * SEQ, cols] = o.astype(BF16)
    s.post(0, Q, j)
    o = s.ao[1, rows]
    w.wait(j, 3)
    m1 = u + (jnp.concatenate([nn(o, w.out[:, n:n + STEP]) for n in range(0, D, STEP)], 1) + p.bias(3))
    w.done(j, 1)
    b = norm_forward(m1, p.gain(1), p.bias(4), s.hat2.at[j], s.inv2.at[j])
    s.b[rows] = b
    s.post(0, U, j)
    w.wait(j, 4)
    for n in range(0, FF, STEP):
        f = nn(b, w.up[:, n:n + STEP]) + p.up(n, n + STEP)
        t = jnp.tanh(0.7978845608 * (f + 0.044715 * f * f * f))
        half = 0.5 * (1.0 + t)
        s.e[rows, n:n + STEP] = (f * half).astype(BF16)
        s.slope[j, :, n:n + STEP] = half + 0.5 * f * (1.0 - t * t) * (
            0.7978845608 + 0.7978845608 * 3 * 0.044715 * f * f)
    w.done(j, 2)
    s.post(0, W, j)
    e = s.e[rows]
    w.wait(j, 5)
    r = jnp.concatenate([nn(e, w.down[:, n:n + STEP]) for n in range(0, D, STEP)], 1)
    w.done(j, 3)
    return m1 + (r + p.bias(5))


def backward(j, dr, w, p, s, t, last):
    rows = slice(j * R, (j + 1) * R)
    dr2 = dr.astype(BF16)
    s.dr[rows] = dr2
    s.post(1, W, j)
    t.add(2 + 5, jnp.sum(dr, 0, keepdims=True))
    w.ready(j, 2)
    for n in range(0, FF, STEP):
        de = nn(dr2, w.up[:, n:n + STEP])
        df = s.slope[j, :, n:n + STEP] * de
        t.add(12 + n // D, jnp.sum(df, 0, keepdims=True), n % D)
        s.df[rows, n:n + STEP] = df.astype(BF16)
    s.post(1, U, j)
    df = s.df[rows]
    w.ready(j, 3)
    db = jnp.concatenate([nn(df, w.down[:, n:n + STEP]) for n in range(0, D, STEP)], 1)
    dm, dgain, dshift = norm_backward(db, p.gain(1), s.hat2.at[j], s.inv2.at[j])
    t.add(1, dgain)
    t.add(2 + 4, dshift)
    dm1 = dr + dm
    dz = dm1.astype(BF16)
    s.dcz[rows, 3 * D:] = dz
    t.add(2 + 3, jnp.sum(dm1, 0, keepdims=True))
    w.ready(j, 1)
    for n in range(0, D, STEP):
        s.dcz[rows, 2 * D + n:2 * D + n + STEP] = nn(dz, w.out[:, n:n + STEP]).astype(BF16)
    nk = keys_of(j)
    ones = lane_masks(1.0, BF16)
    eighth = lane_masks(0.125, BF16)
    eighth32 = lane_masks(0.125, F32)
    for q in range(2):
        drows = slice(j * R + q * SEQ, j * R + (q + 1) * SEQ)
        for g in range(3):
            cols = slice(g * STEP, (g + 1) * STEP)
            do4 = s.dcz[drows, 2 * D + g * STEP:2 * D + (g + 1) * STEP]
            do4 = jnp.concatenate([do4 * m for m in ones], 0)
            q4 = s.dcz[drows, cols]
            q4 = jnp.concatenate([q4 * m for m in eighth], 0)
            dp = nt(s.v[q, 0:nk, cols], do4)
            pr = p_at(s, j)[3 * q + g]
            ds = (pr * (dp - jnp.sum(pr * dp, 0, keepdims=True))).astype(BF16)
            dq4 = tn(ds, s.k[q, 0:nk, cols])
            dq = sum(dq4[h * SEQ:(h + 1) * SEQ] * eighth32[h] for h in range(4))
            t.add(2 + 1, jnp.sum(dq, 0, keepdims=True), g * STEP)
            s.dcz[drows, cols] = dq.astype(BF16)
            dk = nn(ds, q4)
            dv = nn(pr.astype(BF16), do4)
            lo, hi = j * SEQ, (j + 1) * SEQ
            if not last:
                dk = s.dk[q, 0:nk, cols] + dk
                dv = s.dv[q, 0:nk, cols] + dv
            if j:
                s.dk[q, 0:nk, cols] = dk
                s.dv[q, 0:nk, cols] = dv
            s.dcz[drows, D + g * STEP:D + (g + 1) * STEP] = dk[lo:hi].astype(BF16)
            s.dcz[drows, 2 * D + g * STEP:2 * D + (g + 1) * STEP] = dv[lo:hi].astype(BF16)
            t.add(2 + 2, jnp.sum(dv[lo:hi], 0, keepdims=True), g * STEP)
    s.post(1, Q, j)
    dc = s.dcz[rows, 0:3 * D]
    w.ready(j, 0)
    back = w.qkv.reshape(3 * D, D)
    da = jnp.concatenate([nn(dc, back[:, n:n + STEP]) for n in range(0, D, STEP)], 1)
    dx, dgain, dshift = norm_backward(da, p.gain(0), s.hat1.at[j], s.inv1.at[j])
    t.add(0, dgain)
    t.add(2, dshift)
    return dm1 + dx


def slot_rows(j):
    return pl.ds(j * R if isinstance(j, int) else pl.multiple_of(j * R, R), R)


def partner_copy(src, dst, sems):
    return pltpu.make_async_remote_copy(
        src_ref=src, dst_ref=dst, send_sem=sems.at[0], recv_sem=sems.at[1],
        device_id={"section": 1 - lax.axis_index("section")}, device_id_type=MESH)


def rank(axis):
    return lax.rem(lax.div(lax.axis_index("dp"), STRIDE[axis]), 4)


def main_kernel(tokens, out_grad, passes, embed, w_qkv, w_out, w_up, w_down, gains, biases, up_bias,
                keep, got, q_out, o_out, u_out, d_out, sums, sums_other, xs, turned,
                qkv_v, out_v, up_v, down_v, k, v, prob, hat1, inv1, hat2, inv2, slope, dk, dv, state,
                ao, b, e, dcz, df, dr, small, halves, leave, arrive, give, y0, entry,
                q2s, u2s, d2s, d3s, q2r, u2r, d2r, d3r,
                q4s, u4s, q4r, u4r, vec, vec_in,
                wsem, tsem, usem, xsem, hsem, gsem, psem, vsem, psend, precv, plocal, stage, esend, erecv,
                asend, arecv, ssend, srecv):
    sec = lax.axis_index("section")
    dp = lax.axis_index("dp")
    loads = [pltpu.make_async_copy(w_qkv.at[0, :, pl.ds(i * D, D)], qkv_v.at[i], wsem.at[i]) for i in range(3)]
    loads += [pltpu.make_async_copy(src.at[0], dst, wsem.at[3 + i]) for i, (src, dst) in enumerate(
        ((w_out, out_v), (w_up, up_v), (w_down, down_v)))]
    for c in loads:
        c.start()
    ranks = [rank(axis) for axis in AXES]
    peers = [[lax.rem(ranks[g] + by, 4) for by in range(4)] for g in range(3)]
    places = [[dp + (peers[g][by] - ranks[g]) * STRIDE[AXES[g]] for by in range(4)] for g in range(3)]
    offsets = [[pl.multiple_of(peers[g][by] * D, D) for by in range(4)] for g in range(3)]
    seconds = [lax.div(peers[Q][by], 3) for by in range(4)]
    barrier = pltpu.get_barrier_semaphore()
    for g in range(3):
        for by in (1, 2, 3):
            pl.semaphore_signal(barrier, inc=1, device_id={"dp": places[g][by]}, device_id_type=MESH)
            pl.semaphore_signal(barrier, inc=1, device_id={"dp": places[g][by], "section": 1 - sec},
                                device_id_type=MESH)
    planes = {}
    for g, axis in ((U, "y"), (Q, "z")):
        pos = rank(axis)
        planes[g] = [[places[g][by] + (lax.rem(pos + over, 4) - pos) * STRIDE[axis] for by in range(4)]
                     for over in range(4)]
        for over in (1, 2, 3):
            for by in (1, 2, 3):
                pl.semaphore_signal(barrier, inc=1, device_id={"dp": planes[g][over][by]}, device_id_type=MESH)
    pl.semaphore_signal(barrier, inc=1, device_id={"section": 1 - sec}, device_id_type=MESH)
    give[...] = jnp.where(sec == 0, out_grad[...], tokens[...])
    own = jnp.where(sec == 0, tokens[...], out_grad[...])
    pl.semaphore_wait(barrier, 37)
    exchange = partner_copy(give, halves.at[sec], xsem)
    exchange.start()
    halves[sec] = own

    wide = (dcz, df, e)

    def source(which, g, j, by):
        rows = slot_rows(j)
        if g == Q:
            return ao.at[seconds[by], rows] if which == 0 else dcz.at[rows, pl.ds(offsets[g][by], D)]
        if g == U:
            return b.at[rows] if which == 0 else df.at[rows, pl.ds(offsets[g][by], D)]
        return e.at[rows, pl.ds(offsets[g][by], D)] if which == 0 else dr.at[rows]

    def target(which, g, j, by, first):
        if which == 0:
            return xs.at[g, j, peers[g][by]]
        if first:
            return y0.at[g, peers[g][by]]
        return wide[g].at[slot_rows(j), pl.ds(offsets[g][by], D)]

    def remote(which, g, j, by, first):
        return pltpu.make_async_remote_copy(
            src_ref=source(which, g, j, by), dst_ref=target(which, g, j, 0, first),
            send_sem=psend.at[which, g, j, by], recv_sem=precv.at[which, g, j, ranks[g]],
            device_id={"dp": places[g][by], "section": sec if first else 1 - sec}, device_id_type=MESH)

    def inside(which, g):
        return pltpu.make_async_copy(source(which, g, 0, 0), target(which, g, 0, 0, True), plocal.at[which, g])

    def post(which, g, j):
        for by in (2, 1, 3, 0):
            if by or j:
                remote(which, g, j, by, j == 0).start()
        if j == 0:
            inside(which, g).start()

    def arrived(which, g, j, first=False):
        for by in range(1 if first else 0, 4):
            there = target(which, g, j, by, first)
            pltpu.make_async_remote_copy(
                src_ref=there, dst_ref=there, send_sem=psend.at[which, g, 0, 0],
                recv_sem=precv.at[which, g, j, peers[g][by]],
                device_id={"dp": places[g][1]}, device_id_type=MESH).wait_recv()
        if first:
            inside(which, g).wait()

    class Sum:
        def __init__(self, g, m, n):
            if g == Q:
                self.refs = [r.at[1 + m, :, pl.ds(n * STEP, STEP)] for r in (hat1, hat2)]
            else:
                at = 2 * (n + (3 if g == U else 0))
                self.refs = [slope.at[1 + m, :, pl.ds((at + h) * STEP, STEP)] for h in range(2)]

        def read(self):
            return jnp.concatenate([r[...] for r in self.refs], 0)

        def write(self, value):
            size = STEP // len(self.refs)
            for i, r in enumerate(self.refs):
                r[...] = value[i * size:(i + 1) * size]

    tiles = [(m, n) for m in range(3) for n in range(3)]
    stacks = {Q: q2s, U: u2s, W: d2s}
    second = {g: r.reshape(D, D) for g, r in stacks.items()}

    def turn(first):
        blocks = [(qkv_v.at[i], 0) for i in range(3)] + [(out_v, 0)]
        blocks += [(down_v.at[pl.ds(i * D, D)], 0) for i in range(4)] + [(up_v, i * D) for i in range(4)]
        copies = []
        for i, (src, lo) in enumerate(blocks):
            if first:
                for order in {0: (0,), 1: (1,), 2: (2,), 3: (3,), 4: (5,), 8: (4,)}.get(i, ()):
                    loads[order].wait()
            if i >= 3:
                copies[i - 3].wait()
            dst = second[i % 3]
            def flip(m, carry):
                at = pl.multiple_of(m * STEP, STEP)
                for n in range(3):
                    dst[n * STEP:(n + 1) * STEP, pl.ds(at, STEP)] = src[
                        pl.ds(at, STEP), lo + n * STEP:lo + (n + 1) * STEP].T
                return carry
            lax.fori_loop(0, 3, flip, 0)
            copies.append(pltpu.make_async_copy(dst, turned.at[i], tsem.at[i]))
            copies[-1].start()
        for c in copies[-3:]:
            c.wait()

    returns = [[pltpu.make_async_copy(turned.at[pl.ds(0, 3)], qkv_v, usem.at[0])],
               [pltpu.make_async_copy(turned.at[3], out_v, usem.at[1])],
               [pltpu.make_async_copy(turned.at[4 + i], up_v.at[:, pl.ds(i * D, D)], usem.at[2 + i])
                for i in range(4)],
               [pltpu.make_async_copy(turned.at[8 + i], down_v.at[pl.ds(i * D, D)], usem.at[6 + i])
                for i in range(4)]]

    w = Names(qkv=qkv_v, out=out_v, up=up_v, down=down_v)

    def wait(j, i):
        if j == 0 and i not in waited:
            waited.append(i)

            @pl.when(sec == 0)
            def _():
                loads[i].wait()

    def done(j, i):
        if j == SLOTS - 1:
            for c in returns[i]:
                c.start()

    def ready(j, i):
        if j == SLOTS - 1:
            for c in returns[i]:
                c.wait()
    waited = []
    w.wait, w.done, w.ready = wait, done, ready
    p = Names(gain=lambda i: gains[0, i:i + 1, :], bias=lambda i: biases[i],
              up=lambda lo, hi: up_bias[:, lo:hi])
    s = Names(k=k, v=v, p=prob, hat1=hat1, inv1=inv1, hat2=hat2, inv2=inv2, slope=slope, dk=dk, dv=dv,
              ao=ao, b=b, e=e, dcz=dcz, df=df, dr=dr, post=post)
    small[...] = jnp.zeros_like(small)

    def add(i, value, at=0):
        cols = slice(at, at + value.shape[1])
        small[i:i + 1, cols] = small[i:i + 1, cols] + value
    t = Names(add=add)
    k[...] = jnp.zeros_like(k)
    v[...] = jnp.zeros_like(v)
    dk[:, 0:128] = jnp.zeros((2, 128, D), F32)
    dv[:, 0:128] = jnp.zeros((2, 128, D), F32)
    entry[...] = jnp.zeros_like(entry)
    row = lax.broadcasted_iota(jnp.int32, (R, 1), 0)
    count = jnp.where(row < SEQ, passes[0], passes[1]) - 1
    count = jnp.where(sec == 0, SLOTS, count)
    hand = partner_copy(leave, arrive, hsem)
    present = partner_copy(give, got, gsem)
    partial = [partner_copy(r, r, psem.at[i]) for i, r in enumerate((q2s, u2s, d2s))]

    def joined():
        return jnp.concatenate([halves[h, i] for i in range(2) for h in range(2)], 0).astype(F32)

    def step_forward(j, row_of):
        h = state[...]
        r = forward(j, h + row_of, w, p, s)
        state[...] = jnp.where(count > j, r, h)

    def step_backward(j):
        g = state[...]
        du = backward(j, jnp.where(count > j, g, 0.0), w, p, s, t, j == SLOTS - 1)
        entry[j] = jnp.sum(du, 0, keepdims=True)
        state[...] = jnp.where(count > j, du, g)

    @pl.when(sec == 0)
    def _():
        exchange.wait()
        state[...] = joined()

    @pl.when(sec == 1)
    def _():
        turn(True)
        exchange.wait()
        hand.wait_recv()
        state[...] = arrive[...].astype(F32)

    step_forward(0, jnp.where(sec == 0, embed[0:1, :], embed[1:2, :]))

    @pl.when(sec == 0)
    def _():
        leave[...] = state[...].astype(BF16)
        hand.start()
        turn(False)
        for group in returns:
            for c in group:
                c.start()

        def staging(g, j):
            return [pltpu.make_async_copy(xs.at[g, j, i], second[g].at[pl.ds(i * R, R)], stage.at[g, i])
                    for i in range(4)]

        def bring(g, j):
            arrived(0, g, j)
            for c in staging(g, j):
                c.start()

        def clear(m, carry):
            for g in range(3):
                for n in range(3):
                    Sum(g, m, n).write(jnp.zeros((STEP, STEP), F32))
            return carry
        lax.fori_loop(0, 3, clear, 0)
        for g in (W, U, Q):
            bring(g, SLOTS - 1)
        for group in returns:
            for c in group:
                c.wait()

        def gather(i, carry):
            j = SLOTS - 1 - i
            rows = slot_rows(j)
            for g in (W, U, Q):
                for c in staging(g, j):
                    c.wait()
                arrived(1, g, j)

                def across(m, carry):
                    left = second[g][0:ROWS, pl.ds(pl.multiple_of(m * STEP, STEP), STEP)]
                    for n in range(3):
                        right = jnp.concatenate([
                            wide[g][rows, x * D + n * STEP:x * D + (n + 1) * STEP] for x in range(4)], 0)
                        held = Sum(g, m, n)
                        held.write(held.read() + tn(left, right))
                    return carry
                lax.fori_loop(0, 3, across, 0)

                @pl.when(j > 1)
                def _():
                    bring(g, j - 1)

                @pl.when(j == 1)
                def _():
                    def rounded(m, carry):
                        there = pl.ds(pl.multiple_of(m * STEP, STEP), STEP)
                        for n in range(3):
                            second[g][there, n * STEP:(n + 1) * STEP] = Sum(g, m, n).read().astype(BF16)
                        return carry
                    lax.fori_loop(0, 3, rounded, 0)
                    partial[g].start()
            return carry
        lax.fori_loop(0, SLOTS - 1, gather, 0)
        hand.wait()
        state[...] = arrive[...].astype(F32)

    @pl.when(sec == 1)
    def _():
        for j in range(1, SLOTS):
            step_forward(j, embed[j + 1:j + 2, :])
        final = state[...].astype(BF16)
        for i in range(2):
            give[i] = final[i * SEQ:i * SEQ + 32]
            keep[i] = final[i * SEQ + 32:i * SEQ + 64]
        present.start()
        state[...] = joined()
        for j in range(SLOTS - 1, 0, -1):
            step_backward(j)

    step_backward(0)
    fetched = [[pltpu.make_async_copy(xs.at[g, 0, i], up_v.at[pl.ds(i * R, R), pl.ds(g * D, D)], stage.at[g, i])
                for i in range(4)] for g in range(3)]
    for g in (W, U, Q):
        arrived(0, g, 0, True)
        for c in fetched[g]:
            c.start()

    @pl.when(sec == 0)
    def _():
        final = state[...].astype(BF16)
        for i in range(2):
            keep[i] = final[i * SEQ:i * SEQ + 32]
            give[i] = final[i * SEQ + 32:i * SEQ + 64]
        present.start()
        for g in range(3):
            partial[g].wait_send()

    @pl.when(sec == 1)
    def _():
        leave[...] = state[...].astype(BF16)
        hand.start()

    def shares(axis, number):
        pos = rank(axis)
        copies = []
        for by in (1, 2, 3):
            there = dp + (lax.rem(pos + by, 4) - pos) * STRIDE[axis]
            copies.append(pltpu.make_async_remote_copy(
                src_ref=vec.at[number], dst_ref=vec_in.at[number, by - 1], send_sem=ssend.at[number, by - 1],
                recv_sem=srecv.at[number, by - 1], device_id={"dp": there}, device_id_type=MESH))
        return copies
    shared = [shares(axis, number) for number, axis in enumerate(("z", "y", "x"))]

    def share_start(number):
        for c in shared[number]:
            c.start()

    def share_next(number):
        for c in shared[number]:
            c.wait_recv()
        vec[number + 1] = vec[number] + vec_in[number, 0] + vec_in[number, 1] + vec_in[number, 2]
        if number < 2:
            share_start(number + 1)
    vec[0] = small[...]
    for j in range(SLOTS):
        vec[0, 8 + j:9 + j, :] = entry[j]
    share_start(0)

    class Part:
        def __init__(self, axis, number, block, landing):
            self.axis, self.number, self.block, self.landing = axis, number, block, landing
            self.pos = rank(axis)

        def copies(self, c):
            made = []
            for by in (2, 1, 3):
                to = lax.rem(self.pos + by, 4)
                made.append(pltpu.make_async_remote_copy(
                    src_ref=self.block(to, columns(c)), dst_ref=self.landing(by - 1, columns(c)),
                    send_sem=esend.at[self.number, c, by - 1], recv_sem=erecv.at[self.number, c, by - 1],
                    device_id={"dp": dp + (to - self.pos) * STRIDE[self.axis]}, device_id_type=MESH))
            return made

        def start(self, c):
            for copy in self.copies(c):
                copy.start()

        def finish(self, c, store):
            for copy in self.copies(c):
                copy.wait_recv()
            own = self.block(self.pos, columns(c))
            others = [self.landing(i, columns(c)) for i in range(3)]
            for i in range(4 if len(own.shape) == 3 else 1):
                key = (i,) if len(own.shape) == 3 else (slice(None),)
                value = own[key].astype(F32)
                for other in others:
                    value = value + other[key].astype(F32)
                store(i, columns(c), value)

        def drain(self, c):
            for copy in self.copies(c):
                copy.wait_send()

    def columns(c):
        return pl.ds(pl.multiple_of(c * STEP, STEP), STEP)

    d2 = Part("z", 0, lambda i, c: d2s.at[:, i, :, c], lambda i, c: d2r.at[i, :, :, c])
    u2 = Part("x", 1, lambda i, c: u2s.at[:, i, :, c], lambda i, c: u2r.at[i, :, :, c])
    q2 = Part("y", 2, lambda i, c: q2s.at[i, :, c], lambda i, c: q2r.at[i, :, c])
    d3 = Part("x", 3, lambda i, c: d3s.at[i, :, c], lambda i, c: d3r.at[i, :, c])

    def each(body):
        def step(c, carry):
            body(c)
            return carry
        lax.fori_loop(0, 3, step, 0)

    def multiply(g, one):
        for c in fetched[g]:
            c.wait()
        arrived(1, g, 0, True)

        @pl.when(sec == 1)
        def _():
            partial[g].wait_recv()

        def across(c):
            right = y0[g, :, :, columns(c)].reshape(ROWS, STEP)
            for m in range(3):
                part = second[g].at[m * STEP:(m + 1) * STEP, columns(c)]
                held = jnp.where(sec == 1, part[...].astype(F32), 0.0)
                left = up_v[0:ROWS, g * D + m * STEP:g * D + (m + 1) * STEP]
                part[...] = (held + tn(left, right)).astype(BF16)
            one.start(c)
        each(across)

    def to_rows(dst):
        def store(i, at, value):
            dst[i, :, at] = value.astype(BF16)
        return store

    def twelve(rows):
        return jnp.concatenate([rows, jnp.zeros((4, STEP), F32)], 0).astype(BF16)

    def to_plane_u(y, at, value):
        for z in range(4):
            u4s[y, z, :, at] = twelve(value[12 * z:12 * z + 12])

    def to_plane_q(i, at, value):
        for x in range(4):
            for z in range(4):
                q4s[z, x, :, at] = twelve(value[48 * x + 12 * z:48 * x + 12 * z + 12])

    def to_out(i, at, value):
        d_out[:, at] = value

    def plane(g, src, dst):
        axis = "y" if g == U else "z"
        pos = rank(axis)
        return [pltpu.make_async_remote_copy(
            src_ref=src.at[lax.rem(pos + over, 4), peers[g][by]], dst_ref=dst.at[over, ranks[g]],
            send_sem=asend.at[g, over, by], recv_sem=arecv.at[g, over, ranks[g]],
            device_id={"dp": planes[g][over][by]}, device_id_type=MESH)
            for over in range(4) for by in range(4) if over or by]

    def plane_sum(g, dst, r):
        value = dst[0, r].astype(F32)
        for over in (1, 2, 3):
            value = value + dst[over, r].astype(F32)
        return value[0:12]

    def plane_arrived(g, dst):
        for over in range(4):
            for by in range(4):
                if over or by:
                    there = dst.at[over, peers[g][by]]
                    pltpu.make_async_remote_copy(
                        src_ref=there, dst_ref=there, send_sem=asend.at[g, 0, 0],
                        recv_sem=arecv.at[g, over, peers[g][by]],
                        device_id={"dp": places[g][1]}, device_id_type=MESH).wait_recv()

    multiply(W, d2)
    multiply(U, u2)
    multiply(Q, q2)
    share_next(0)

    for which in range(2):
        for g in range(3):
            for by in (1, 2, 3):
                remote(which, g, 0, by, True).wait_send()

    @pl.when(sec == 1)
    def _():
        hand.wait_send()

        def drain(j, carry):
            for which in range(2):
                for g in range(3):
                    for by in range(4):
                        remote(which, g, j, by, False).wait_send()
            return carry
        lax.fori_loop(1, SLOTS, drain, 0)
    present.wait()

    def second_done(c):
        u2.finish(c, to_plane_u)
        d2.finish(c, to_rows(d3s))
        d3.start(c)
    each(second_done)
    spread_u = plane(U, u4s, u4r)
    for copy in spread_u:
        copy.start()
    u4r[0, ranks[U]] = u4s[rank("y"), ranks[U]]
    each(lambda c: q2.finish(c, to_plane_q))
    spread_q = plane(Q, q4s, q4r)
    for copy in spread_q:
        copy.start()
    q4r[0, ranks[Q]] = q4s[rank("z"), ranks[Q]]
    share_next(1)

    def drained(c):
        for one in (d2, u2, q2):
            one.drain(c)
    each(drained)
    each(lambda c: d3.finish(c, to_out))
    share_next(2)
    sums[...] = vec[3]
    other = partner_copy(vec.at[3], sums_other, vsem)
    other.start()
    plane_arrived(U, u4r)
    for i in range(4):
        u_out[:, i * D:(i + 1) * D] = plane_sum(U, u4r, i)
    plane_arrived(Q, q4r)
    for i in range(3):
        q_out[:, i * D:(i + 1) * D] = plane_sum(Q, q4r, i)
    o_out[...] = plane_sum(Q, q4r, 3)
    each(lambda c: d3.drain(c))
    for copies in shared + [spread_u, spread_q]:
        for copy in copies:
            copy.wait_send()
    other.wait()


def main(*args):
    vmem = pl.BlockSpec(memory_space=VM)
    hbm = pl.BlockSpec(memory_space=pltpu.HBM)
    dma = pltpu.SemaphoreType.DMA
    return pl.pallas_call(
        main_kernel,
        out_shape=[jax.ShapeDtypeStruct(dims, dtype) for dims, dtype in (
            ((2, 32, D), BF16), ((2, 32, D), BF16), ((12, 3 * D), F32), ((12, D), F32), ((12, FF), F32), ((48, D), F32),
            ((16, D), F32), ((16, D), F32), ((3, SLOTS, 4, R, D), BF16), ((12, D, D), BF16))],
        in_specs=[vmem, vmem, pl.BlockSpec(memory_space=pltpu.SMEM), vmem] + [hbm] * 4 + [vmem] * 3,
        out_specs=[vmem] * 8 + [hbm] * 2,
        scratch_shapes=[
            VM((3, D, D), BF16), VM((D, D), BF16), VM((D, FF), BF16), VM((FF, D), BF16),
            VM((2, 256, D), BF16), VM((2, 256, D), BF16), VM((SLOTS - 1, 6, 256, 256), F32),
            VM((SLOTS, R, D), F32), VM((SLOTS, R, 128), F32), VM((SLOTS, R, D), F32), VM((SLOTS, R, 128), F32),
            VM((SLOTS, R, FF), F32), VM((2, 256, D), F32), VM((2, 256, D), F32), VM((R, D), F32),
            VM((2, ROWS, D), BF16), VM((ROWS, D), BF16), VM((ROWS, FF), BF16), VM((ROWS, 4 * D), BF16),
            VM((ROWS, FF), BF16), VM((ROWS, D), BF16), VM((16, D), F32),
            VM((2, 2, 32, D), BF16), VM((R, D), BF16), VM((R, D), BF16), VM((2, 32, D), BF16),
            VM((3, 4, R, D), BF16), VM((SLOTS, 1, D), F32),
            VM((4, 192, D), BF16), VM((4, 4, 48, D), BF16), VM((4, 4, 48, D), BF16),
            VM((4, 48, D), BF16),
            VM((3, 192, D), BF16), VM((3, 4, 48, D), BF16), VM((3, 4, 48, D), BF16),
            VM((3, 48, D), BF16)]
        + [VM((4, 4, 16, D), BF16)] * 4 + [VM((4, 16, D), F32), VM((3, 3, 16, D), F32)]
        + [dma((6,)), dma((12,)), dma((10,)), dma((2,)), dma((2,)), dma((2,)), dma((3, 2)), dma((2,)),
           dma((2, 3, SLOTS, 4)), dma((2, 3, SLOTS, 4)), dma((2, 3)), dma((3, 4)), dma((4, 3, 3)), dma((4, 3, 3)),
           dma((2, 4, 4)), dma((2, 4, 4)), dma((3, 3)), dma((3, 3))],
        compiler_params=pltpu.CompilerParams(collective_id=0, has_side_effects=True, vmem_limit_bytes=int(63.4 * 2**20)),
        name="layers",
    )(*args)


def finish_kernel(keep, got, q_in, o_in, u_in, d_in, sums, other,
                  hidden, token, q_out, o_out, u_out, d_out, g_gains, g_bias, g_up, g_embed):
    sec = lax.axis_index("section")
    dp = lax.axis_index("dp")
    hidden[...] = jnp.where(sec == 0, got[...], keep[...])
    token[...] = jnp.where(sec == 0, keep[...], got[...])
    for i in range(12):
        q_out[i] = q_in[i:i + 1, :]
        o_out[i] = o_in[i:i + 1, :]
        u_out[i] = u_in[i:i + 1, :]
    d_out[0] = d_in[...]
    turned = pltpu.roll(sums[...], lax.rem(D - dp * 12, D), 1)
    g_gains[0] = turned[0:2, 0:12]
    for i in range(6):
        g_bias[i] = turned[2 + i:3 + i, 0:12]
    lines = sums[12:13, :]
    for i in range(1, 4):
        lines = jnp.where(lax.div(dp, 16) == i, sums[12 + i:13 + i, :], lines)
    g_up[...] = pltpu.roll(lines, lax.rem(D - lax.rem(dp, 16) * 48, D), 1)[:, 0:48]
    mine, theirs = sums[8:12, :], other[8:12, :]
    rows = jnp.concatenate([jnp.where(sec == 0, mine, theirs)[0:1], jnp.where(sec == 0, theirs, mine)], 0)
    g_embed[...] = pltpu.roll(rows, lax.rem(D - (sec * 64 + dp) * 6, D), 1)[:, 0:6]


def finish(*args):
    vmem = pl.BlockSpec(memory_space=VM)
    return pl.pallas_call(
        finish_kernel,
        out_shape=[jax.ShapeDtypeStruct(dims, dtype) for dims, dtype in (
            ((2, 32, D), BF16), ((2, 32, D), BF16), ((12, 1, 3 * D), F32), ((12, 1, D), F32), ((12, 1, FF), F32),
            ((1, 48, D), F32), ((1, 2, 12), F32), ((6, 1, 12), F32), ((1, 48), F32), ((5, 6), F32))],
        in_specs=[vmem] * 8, out_specs=[vmem] * 10,
        name="finish",
    )(*args)


def local(*args):
    args = list(args)
    args[9] = jnp.swapaxes(args[9], 0, 1)
    outs = list(finish(*main(*args)[:8]))
    for i in (2, 3, 4, 7):
        outs[i] = jnp.swapaxes(outs[i], 0, 1)
    return tuple(outs)


def solution(mesh):
    split = ("section",)
    placed = (
        P("dp", "section", None), P("dp", "section", None), P("dp"), P(),
        P("section", None, None), P("section", None, None), P("section", None, None), P("section", None, None),
        P("section", None, None), P("section", None, None), P("section", None))
    return jax.shard_map(
        local, mesh=mesh, in_specs=placed,
        out_specs=(
            P("dp", "section", None), P("dp", "section", None),
            P("section", "dp", None), P("section", "dp", None), P("section", "dp", None), P("section", "dp", None),
            P("section", None, "dp"), P("section", None, "dp"), P("section", "dp"), P(None, ("section", "dp"))),
        check_vma=False)
```

```python
import jax
import jax.numpy as jnp
import numpy as np
from jax import lax
from jax.experimental import pallas as pl
from jax.experimental.pallas import tpu as pltpu
from jax.sharding import PartitionSpec as P

F32 = jnp.float32
BF16 = jnp.bfloat16
VM = pltpu.VMEM
MESH = pl.DeviceIdType.MESH
D = 768
FF = 3072
SEQ = 64
R = 2 * SEQ
SLOTS = 4
ROWS = SLOTS * R
STEP = 256
KEYS = SLOTS * SEQ
STRIDE = {"y": 16, "x": 4, "z": 1}
Q, U, W = 0, 1, 2
AXES = ("x", "z", "y")


class Names:
    def __init__(self, **entries):
        self.__dict__.update(entries)


def nn(a, b):
    return jnp.dot(a, b, preferred_element_type=F32)


def nt(a, b):
    return lax.dot_general(a, b, (((1,), (1,)), ((), ())), preferred_element_type=F32)


def tn(a, b):
    return lax.dot_general(a, b, (((0,), (0,)), ((), ())), preferred_element_type=F32)


def lane_masks(value, dtype):
    lane = lax.broadcasted_iota(jnp.int32, (1, STEP), 1) // 64
    return [jnp.where(lane == h, value, 0.0).astype(dtype) for h in range(4)]


def norm_forward(u, gain, shift, hat_ref, inv_ref):
    out = []
    for r in range(0, R, 32):
        v = u[r:r + 32]
        centre = v - jnp.sum(v, -1, keepdims=True) * (1.0 / D)
        inv = lax.rsqrt(jnp.sum(centre * centre, -1, keepdims=True) * (1.0 / D) + 1e-5)
        hat = centre * inv
        hat_ref[r:r + 32] = hat
        inv_ref[r:r + 32] = jnp.broadcast_to(inv, (32, 128))
        out.append((hat * gain + shift).astype(BF16))
    return jnp.concatenate(out, 0)


def norm_backward(dy, gain, hat_ref, inv_ref):
    out, dgain, dshift = [], 0.0, 0.0
    for r in range(0, R, 32):
        g = dy[r:r + 32]
        hat = hat_ref[r:r + 32]
        inv = inv_ref[r:r + 32][:, :1]
        dgain = dgain + jnp.sum(g * hat, 0, keepdims=True)
        dshift = dshift + jnp.sum(g, 0, keepdims=True)
        gg = g * gain
        m1 = jnp.sum(gg, -1, keepdims=True) * (1.0 / D)
        m2 = jnp.sum(gg * hat, -1, keepdims=True) * (1.0 / D)
        out.append((gg - m1 - hat * m2) * inv)
    return jnp.concatenate(out, 0), dgain, dshift


def forward(j, u, w, p, s):
    rows = pl.ds(pl.multiple_of(j * R, R), R)
    slot = pl.ds(pl.multiple_of(j * SEQ, SEQ), SEQ)
    a = norm_forward(u, p.gain(0), p.bias(0), s.hat1.at[j], s.inv1.at[j])
    s.ao[0, rows] = a
    for n in range(0, 3 * D, STEP):
        k = n % D
        if k == 0:
            w.wait(j, n // D)
        c = nn(a, w.qkv[n // D, :, k:k + STEP])
        if n < D:
            s.dcz[rows, k:k + STEP] = (c + p.bias(1)[:, k:k + STEP]).astype(BF16)
        elif n < 2 * D:
            c = c.astype(BF16)
            for q in range(2):
                s.k[q, slot, k:k + STEP] = c[q * SEQ:(q + 1) * SEQ]
        else:
            c = (c + p.bias(2)[:, k:k + STEP]).astype(BF16)
            for q in range(2):
                s.v[q, slot, k:k + STEP] = c[q * SEQ:(q + 1) * SEQ]
    w.done(j, 0)
    ones = lane_masks(1.0, F32)
    eighth = lane_masks(0.125, BF16)
    key = lax.broadcasted_iota(jnp.int32, (KEYS, STEP), 0)
    place = lax.broadcasted_iota(jnp.int32, (KEYS, STEP), 1) & 63
    allow = ((key & 63) <= place) & (key < (j + 1) * SEQ)
    veto = jnp.where(allow, 0.0, -1e30)
    for q in range(2):
        qrows = pl.ds(pl.multiple_of(j * R + q * SEQ, SEQ), SEQ)
        for g in range(3):
            cols = slice(g * STEP, (g + 1) * STEP)
            q4 = s.dcz[qrows, cols]
            q4 = jnp.concatenate([q4 * m for m in eighth], 0)
            sc = nt(s.k[q, :, cols], q4) + veto
            ex = jnp.exp(sc - jnp.max(sc, 0, keepdims=True))
            pr = ex * (1.0 / jnp.sum(ex, 0, keepdims=True))
            s.p[j, 3 * q + g] = pr
            o4 = tn(pr.astype(BF16), s.v[q, :, cols])
            o = sum(o4[h * SEQ:(h + 1) * SEQ] * ones[h] for h in range(4))
            s.ao[1, qrows, cols] = o.astype(BF16)
    s.post(0, Q, j)
    o = s.ao[1, rows]
    w.wait(j, 3)
    m1 = u + (jnp.concatenate([nn(o, w.out[:, n:n + STEP]) for n in range(0, D, STEP)], 1) + p.bias(3))
    w.done(j, 1)
    b = norm_forward(m1, p.gain(1), p.bias(4), s.hat2.at[j], s.inv2.at[j])
    s.b[rows] = b
    s.post(0, U, j)
    w.wait(j, 4)
    for n in range(0, FF, STEP):
        f = nn(b, w.up[:, n:n + STEP]) + p.up(n, n + STEP)
        t = jnp.tanh(0.7978845608 * (f + 0.044715 * f * f * f))
        half = 0.5 * (1.0 + t)
        s.e[rows, n:n + STEP] = (f * half).astype(BF16)
        s.slope[j, :, n:n + STEP] = half + 0.5 * f * (1.0 - t * t) * (
            0.7978845608 + 0.7978845608 * 3 * 0.044715 * f * f)
    w.done(j, 2)
    s.post(0, W, j)
    e = s.e[rows]
    w.wait(j, 5)
    r = jnp.concatenate([nn(e, w.down[:, n:n + STEP]) for n in range(0, D, STEP)], 1)
    w.done(j, 3)
    return m1 + (r + p.bias(5))


def backward(j, dr, w, p, s, t):
    rows = pl.ds(pl.multiple_of(j * R, R), R)
    slot = pl.ds(pl.multiple_of(j * SEQ, SEQ), SEQ)
    dr2 = dr.astype(BF16)
    s.dr[rows] = dr2
    s.post(1, W, j)
    t.add(2 + 5, jnp.sum(dr, 0, keepdims=True))
    w.ready(j, 2)
    for n in range(0, FF, STEP):
        de = nn(dr2, w.up[:, n:n + STEP])
        df = s.slope[j, :, n:n + STEP] * de
        t.add(12 + n // D, jnp.sum(df, 0, keepdims=True), n % D)
        s.df[rows, n:n + STEP] = df.astype(BF16)
    s.post(1, U, j)
    df = s.df[rows]
    w.ready(j, 3)
    db = jnp.concatenate([nn(df, w.down[:, n:n + STEP]) for n in range(0, D, STEP)], 1)
    dm, dgain, dshift = norm_backward(db, p.gain(1), s.hat2.at[j], s.inv2.at[j])
    t.add(1, dgain)
    t.add(2 + 4, dshift)
    dm1 = dr + dm
    dz = dm1.astype(BF16)
    s.dcz[rows, 3 * D:] = dz
    t.add(2 + 3, jnp.sum(dm1, 0, keepdims=True))
    w.ready(j, 1)
    for n in range(0, D, STEP):
        s.dcz[rows, 2 * D + n:2 * D + n + STEP] = nn(dz, w.out[:, n:n + STEP]).astype(BF16)
    ones = lane_masks(1.0, BF16)
    eighth = lane_masks(0.125, BF16)
    eighth32 = lane_masks(0.125, F32)
    for q in range(2):
        drows = pl.ds(pl.multiple_of(j * R + q * SEQ, SEQ), SEQ)
        for g in range(3):
            cols = slice(g * STEP, (g + 1) * STEP)
            do4 = s.dcz[drows, 2 * D + g * STEP:2 * D + (g + 1) * STEP]
            do4 = jnp.concatenate([do4 * m for m in ones], 0)
            q4 = s.dcz[drows, cols]
            q4 = jnp.concatenate([q4 * m for m in eighth], 0)
            dp = nt(s.v[q, :, cols], do4)
            pr = s.p[j, 3 * q + g]
            ds = (pr * (dp - jnp.sum(pr * dp, 0, keepdims=True))).astype(BF16)
            dq4 = tn(ds, s.k[q, :, cols])
            dq = sum(dq4[h * SEQ:(h + 1) * SEQ] * eighth32[h] for h in range(4))
            t.add(2 + 1, jnp.sum(dq, 0, keepdims=True), g * STEP)
            s.dcz[drows, cols] = dq.astype(BF16)
            s.dk[q, :, cols] = s.dk[q, :, cols] + nn(ds, q4)
            s.dv[q, :, cols] = s.dv[q, :, cols] + nn(pr.astype(BF16), do4)
            s.dcz[drows, D + g * STEP:D + (g + 1) * STEP] = s.dk[q, slot, cols].astype(BF16)
            dv = s.dv[q, slot, cols]
            s.dcz[drows, 2 * D + g * STEP:2 * D + (g + 1) * STEP] = dv.astype(BF16)
            t.add(2 + 2, jnp.sum(dv, 0, keepdims=True), g * STEP)
    s.post(1, Q, j)
    dc = s.dcz[rows, 0:3 * D]
    w.ready(j, 0)
    back = w.qkv.reshape(3 * D, D)
    da = jnp.concatenate([nn(dc, back[:, n:n + STEP]) for n in range(0, D, STEP)], 1)
    dx, dgain, dshift = norm_backward(da, p.gain(0), s.hat1.at[j], s.inv1.at[j])
    t.add(0, dgain)
    t.add(2, dshift)
    return dm1 + dx


def partner_copy(src, dst, sems):
    return pltpu.make_async_remote_copy(
        src_ref=src, dst_ref=dst, send_sem=sems.at[0], recv_sem=sems.at[1],
        device_id={"section": 1 - lax.axis_index("section")}, device_id_type=MESH)


def rank(axis):
    return lax.rem(lax.div(lax.axis_index("dp"), STRIDE[axis]), 4)


def main_kernel(tokens, out_grad, passes, embed, w_qkv, w_out, w_up, w_down, gains, biases, up_bias,
                keep, got, q_out, o_out, u_out, d_out, sums, sums_other, xs, turned,
                qkv_v, out_v, up_v, down_v, k, v, prob, hat1, inv1, hat2, inv2, slope, dk, dv, state,
                ao, b, e, dcz, df, dr, small, halves, leave, arrive, give, entry,
                q2s, u2s, d2s, d3s, q2r, u2r, d2r, d3r,
                q4s, u4s, q4r, u4r, vec, vec_in,
                wsem, tsem, usem, xsem, hsem, gsem, psem, vsem, psend, precv, stage, esend, erecv,
                asend, arecv, ssend, srecv):
    sec = lax.axis_index("section")
    dp = lax.axis_index("dp")
    loads = [pltpu.make_async_copy(w_qkv.at[0, :, pl.ds(i * D, D)], qkv_v.at[i], wsem.at[i]) for i in range(3)]
    loads += [pltpu.make_async_copy(src.at[0], dst, wsem.at[3 + i]) for i, (src, dst) in enumerate(
        ((w_out, out_v), (w_up, up_v), (w_down, down_v)))]
    for c in loads:
        c.start()
    ranks = [rank(axis) for axis in AXES]
    peers = [[lax.rem(ranks[g] + by, 4) for by in range(4)] for g in range(3)]
    places = [[dp + (peers[g][by] - ranks[g]) * STRIDE[AXES[g]] for by in range(4)] for g in range(3)]
    offsets = [[pl.multiple_of(peers[g][by] * D, D) for by in range(4)] for g in range(3)]
    seconds = [lax.div(peers[Q][by], 3) for by in range(4)]
    barrier = pltpu.get_barrier_semaphore()
    for g in range(3):
        for by in (1, 2, 3):
            pl.semaphore_signal(barrier, inc=1, device_id={"dp": places[g][by]}, device_id_type=MESH)
            pl.semaphore_signal(barrier, inc=1, device_id={"dp": places[g][by], "section": 1 - sec},
                                device_id_type=MESH)
    planes = {}
    for g, axis in ((U, "y"), (Q, "z")):
        pos = rank(axis)
        planes[g] = [[places[g][by] + (lax.rem(pos + over, 4) - pos) * STRIDE[axis] for by in range(4)]
                     for over in range(4)]
        for over in (1, 2, 3):
            for by in (1, 2, 3):
                pl.semaphore_signal(barrier, inc=1, device_id={"dp": planes[g][over][by]}, device_id_type=MESH)
    pl.semaphore_signal(barrier, inc=1, device_id={"section": 1 - sec}, device_id_type=MESH)
    give[...] = jnp.where(sec == 0, out_grad[...], tokens[...])
    own = jnp.where(sec == 0, tokens[...], out_grad[...])
    pl.semaphore_wait(barrier, 37)
    exchange = partner_copy(give, halves.at[sec], xsem)
    exchange.start()
    halves[sec] = own

    wide = (dcz, df, e)

    def source(which, g, j, by):
        rows = pl.ds(pl.multiple_of(j * R, R), R)
        if g == Q:
            return ao.at[seconds[by], rows] if which == 0 else dcz.at[rows, pl.ds(offsets[g][by], D)]
        if g == U:
            return b.at[rows] if which == 0 else df.at[rows, pl.ds(offsets[g][by], D)]
        return e.at[rows, pl.ds(offsets[g][by], D)] if which == 0 else dr.at[rows]

    def slot_of(j):
        return jnp.where(j == 0, SLOTS, j)

    def landing(which, g, j, at, spare=False):
        if which == 0:
            return xs.at[g, slot_of(j) if spare else j, at]
        rows = pl.ds(pl.multiple_of(slot_of(j) * R, R), R)
        return wide[g].at[rows, pl.ds(pl.multiple_of(at * D, D), D)]

    def remote(which, g, j, by):
        place, mark, at = places[g][by], ranks[g], ranks[g]
        if by == 0:
            place = jnp.where(j == 0, places[g][1], dp)
            mark = jnp.where(j == 0, peers[g][1], ranks[g])
            at = ranks[g] if which == 0 else mark
        return pltpu.make_async_remote_copy(
            src_ref=source(which, g, j, by), dst_ref=landing(which, g, j, at, by == 0),
            send_sem=psend.at[which, g, j, by], recv_sem=precv.at[which, g, j, mark],
            device_id={"dp": place, "section": jnp.where(j == 0, sec, 1 - sec)}, device_id_type=MESH)

    def post(which, g, j):
        for by in (2, 1, 3, 0):
            remote(which, g, j, by).start()

    def arrived(which, g, j):
        for by in range(4):
            at = peers[g][by]
            if by == 0 and which == 0:
                at = jnp.where(j == 0, peers[g][3], ranks[g])
            there = landing(which, g, j, at, by == 0)
            pltpu.make_async_remote_copy(
                src_ref=there, dst_ref=there, send_sem=psend.at[which, g, 0, 0],
                recv_sem=precv.at[which, g, j, peers[g][by]],
                device_id={"dp": places[g][1]}, device_id_type=MESH).wait_recv()

    class Sum:
        def __init__(self, g, m, n):
            if g == Q:
                self.refs = [r.at[1 + m, :, pl.ds(n * STEP, STEP)] for r in (hat1, hat2)]
            else:
                at = 2 * (n + (3 if g == U else 0))
                self.refs = [slope.at[1 + m, :, pl.ds((at + h) * STEP, STEP)] for h in range(2)]

        def read(self):
            return jnp.concatenate([r[...] for r in self.refs], 0)

        def write(self, value):
            size = STEP // len(self.refs)
            for i, r in enumerate(self.refs):
                r[...] = value[i * size:(i + 1) * size]

    tiles = [(m, n) for m in range(3) for n in range(3)]
    stacks = {Q: q2s, U: u2s, W: d2s}
    second = {g: r.reshape(D, D) for g, r in stacks.items()}

    def turn(first):
        blocks = [(qkv_v.at[i], 0) for i in range(3)] + [(out_v, 0)]
        blocks += [(down_v.at[pl.ds(i * D, D)], 0) for i in range(4)] + [(up_v, i * D) for i in range(4)]
        copies = []
        for i, (src, lo) in enumerate(blocks):
            if first:
                for order in {0: (0,), 1: (1,), 2: (2,), 3: (3,), 4: (5,), 8: (4,)}.get(i, ()):
                    loads[order].wait()
            if i >= 3:
                copies[i - 3].wait()
            dst = second[i % 3]
            def flip(m, carry):
                at = pl.multiple_of(m * STEP, STEP)
                for n in range(3):
                    dst[n * STEP:(n + 1) * STEP, pl.ds(at, STEP)] = src[
                        pl.ds(at, STEP), lo + n * STEP:lo + (n + 1) * STEP].T
                return carry
            lax.fori_loop(0, 3, flip, 0)
            copies.append(pltpu.make_async_copy(dst, turned.at[i], tsem.at[i]))
            copies[-1].start()
        for c in copies[-3:]:
            c.wait()

    returns = [[pltpu.make_async_copy(turned.at[pl.ds(0, 3)], qkv_v, usem.at[0])],
               [pltpu.make_async_copy(turned.at[3], out_v, usem.at[1])],
               [pltpu.make_async_copy(turned.at[4 + i], up_v.at[:, pl.ds(i * D, D)], usem.at[2 + i])
                for i in range(4)],
               [pltpu.make_async_copy(turned.at[8 + i], down_v.at[pl.ds(i * D, D)], usem.at[6 + i])
                for i in range(4)]]

    w = Names(qkv=qkv_v, out=out_v, up=up_v, down=down_v)

    def wait(j, i):
        if i == 3:
            @pl.when((j == 0) & (sec == 0))
            def _():
                for c in loads[3:]:
                    c.wait()

    def done(j, i):
        if i == 2:
            @pl.when(j == SLOTS - 1)
            def _():
                for group in (returns[2], returns[1], returns[0]):
                    for c in group:
                        c.start()

    def ready(j, i):
        if i == 3:
            @pl.when(j == SLOTS - 1)
            def _():
                for group in (returns[3], returns[1], returns[0]):
                    for c in group:
                        c.wait()
    w.wait, w.done, w.ready = wait, done, ready
    p = Names(gain=lambda i: gains[0, i:i + 1, :], bias=lambda i: biases[i],
              up=lambda lo, hi: up_bias[:, lo:hi])
    s = Names(k=k, v=v, p=prob, hat1=hat1, inv1=inv1, hat2=hat2, inv2=inv2, slope=slope, dk=dk, dv=dv,
              ao=ao, b=b, e=e, dcz=dcz, df=df, dr=dr, post=post)
    small[...] = jnp.zeros_like(small)

    def add(i, value, at=0):
        cols = slice(at, at + value.shape[1])
        small[i:i + 1, cols] = small[i:i + 1, cols] + value
    t = Names(add=add)
    k[...] = jnp.zeros_like(k)
    v[...] = jnp.zeros_like(v)
    dk[...] = jnp.zeros_like(dk)
    dv[...] = jnp.zeros_like(dv)
    row = lax.broadcasted_iota(jnp.int32, (R, 1), 0)
    count = jnp.where(row < SEQ, passes[0], passes[1]) - 1
    count = jnp.where(sec == 0, SLOTS, count)
    hand = partner_copy(leave, arrive, hsem)
    present = partner_copy(give, got, gsem)
    partial = [partner_copy(r, r, psem.at[i]) for i, r in enumerate((q2s, u2s, d2s))]

    def joined():
        return jnp.concatenate([halves[h, i] for i in range(2) for h in range(2)], 0).astype(F32)

    slots = jnp.where(sec == 0, 1, SLOTS)

    def step_forward(j, carry):
        h = state[...]
        r = forward(j, h + embed[pl.ds(j + sec, 1), :], w, p, s)
        state[...] = jnp.where(count > j, r, h)
        return carry

    def step_backward(i, carry):
        j = slots - 1 - i
        g = state[...]
        du = backward(j, jnp.where(count > j, g, 0.0), w, p, s, t)
        entry[j] = jnp.sum(du, 0, keepdims=True)
        state[...] = jnp.where(count > j, du, g)
        return carry

    @pl.when(sec == 0)
    def _():
        exchange.wait()
        state[...] = joined()
        for c in loads[:3]:
            c.wait()

    @pl.when(sec == 1)
    def _():
        turn(True)
        exchange.wait()
        hand.wait_recv()
        state[...] = arrive[...].astype(F32)

    lax.fori_loop(0, slots, step_forward, 0)

    @pl.when(sec == 0)
    def _():
        leave[...] = state[...].astype(BF16)
        hand.start()
        turn(False)
        for group in returns:
            for c in group:
                c.start()

        def staging(g, j):
            return [pltpu.make_async_copy(xs.at[g, j, i], second[g].at[pl.ds(i * R, R)], stage.at[g, i])
                    for i in range(4)]

        def bring(g, j):
            arrived(0, g, j)
            for c in staging(g, j):
                c.start()

        def clear(m, carry):
            for g in range(3):
                for n in range(3):
                    Sum(g, m, n).write(jnp.zeros((STEP, STEP), F32))
            return carry
        lax.fori_loop(0, 3, clear, 0)
        for g in (W, U, Q):
            bring(g, SLOTS - 1)
        for group in returns:
            for c in group:
                c.wait()

        def gather(i, carry):
            j = SLOTS - 1 - i
            rows = pl.ds(pl.multiple_of(j * R, R), R)
            for g in (W, U, Q):
                for c in staging(g, j):
                    c.wait()
                arrived(1, g, j)

                def across(m, carry):
                    left = second[g][0:ROWS, pl.ds(pl.multiple_of(m * STEP, STEP), STEP)]
                    for n in range(3):
                        right = jnp.concatenate([
                            wide[g][rows, x * D + n * STEP:x * D + (n + 1) * STEP] for x in range(4)], 0)
                        held = Sum(g, m, n)
                        held.write(held.read() + tn(left, right))
                    return carry
                lax.fori_loop(0, 3, across, 0)

                @pl.when(j > 1)
                def _():
                    bring(g, j - 1)

                @pl.when(j == 1)
                def _():
                    def rounded(m, carry):
                        there = pl.ds(pl.multiple_of(m * STEP, STEP), STEP)
                        for n in range(3):
                            second[g][there, n * STEP:(n + 1) * STEP] = Sum(g, m, n).read().astype(BF16)
                        return carry
                    lax.fori_loop(0, 3, rounded, 0)
                    partial[g].start()
            return carry
        lax.fori_loop(0, SLOTS - 1, gather, 0)
        hand.wait()
        state[...] = arrive[...].astype(F32)

    @pl.when(sec == 1)
    def _():
        for c in returns[3]:
            c.start()
        final = state[...].astype(BF16)
        for i in range(2):
            give[i] = final[i * SEQ:i * SEQ + 32]
            keep[i] = final[i * SEQ + 32:i * SEQ + 64]
        present.start()
        state[...] = joined()
        for c in returns[2]:
            c.wait()

    lax.fori_loop(0, slots, step_backward, 0)
    fetched = [[pltpu.make_async_copy(
        xs.at[g, 0, peers[g][by]] if by else source(0, g, 0, 0),
        up_v.at[pl.ds(by * R, R), pl.ds(g * D, D)], stage.at[g, by]) for by in range(4)] for g in range(3)]
    for g in (W, U, Q):
        arrived(0, g, 0)
        for c in fetched[g]:
            c.start()

    @pl.when(sec == 0)
    def _():
        final = state[...].astype(BF16)
        for i in range(2):
            keep[i] = final[i * SEQ:i * SEQ + 32]
            give[i] = final[i * SEQ + 32:i * SEQ + 64]
        present.start()
        for g in range(3):
            partial[g].wait_send()

    @pl.when(sec == 1)
    def _():
        leave[...] = state[...].astype(BF16)
        hand.start()

    def shares(axis, number):
        pos = rank(axis)
        copies = []
        for by in (1, 2, 3):
            there = dp + (lax.rem(pos + by, 4) - pos) * STRIDE[axis]
            copies.append(pltpu.make_async_remote_copy(
                src_ref=vec.at[number], dst_ref=vec_in.at[number, by - 1], send_sem=ssend.at[number, by - 1],
                recv_sem=srecv.at[number, by - 1], device_id={"dp": there}, device_id_type=MESH))
        return copies
    shared = [shares(axis, number) for number, axis in enumerate(("z", "y", "x"))]

    def share_start(number):
        for c in shared[number]:
            c.start()

    def share_next(number):
        for c in shared[number]:
            c.wait_recv()
        vec[number + 1] = vec[number] + vec_in[number, 0] + vec_in[number, 1] + vec_in[number, 2]
        if number < 2:
            share_start(number + 1)
    vec[0] = small[...]
    for j in range(SLOTS):
        vec[0, 8 + j:9 + j, :] = entry[j]
    share_start(0)

    class Part:
        def __init__(self, axis, number, block, landing):
            self.axis, self.number, self.block, self.landing = axis, number, block, landing
            self.pos = rank(axis)

        def copies(self, c):
            made = []
            for by in (2, 1, 3):
                to = lax.rem(self.pos + by, 4)
                made.append(pltpu.make_async_remote_copy(
                    src_ref=self.block(to, columns(c)), dst_ref=self.landing(by - 1, columns(c)),
                    send_sem=esend.at[self.number, c, by - 1], recv_sem=erecv.at[self.number, c, by - 1],
                    device_id={"dp": dp + (to - self.pos) * STRIDE[self.axis]}, device_id_type=MESH))
            return made

        def start(self, c):
            for copy in self.copies(c):
                copy.start()

        def finish(self, c, store):
            for copy in self.copies(c):
                copy.wait_recv()
            own = self.block(self.pos, columns(c))
            others = [self.landing(i, columns(c)) for i in range(3)]
            for i in range(4 if len(own.shape) == 3 else 1):
                key = (i,) if len(own.shape) == 3 else (slice(None),)
                value = own[key].astype(F32)
                for other in others:
                    value = value + other[key].astype(F32)
                store(i, columns(c), value)

        def drain(self, c):
            for copy in self.copies(c):
                copy.wait_send()

    def columns(c):
        return pl.ds(pl.multiple_of(c * STEP, STEP), STEP)

    d2 = Part("z", 0, lambda i, c: d2s.at[:, i, :, c], lambda i, c: d2r.at[i, :, :, c])
    u2 = Part("x", 1, lambda i, c: u2s.at[:, i, :, c], lambda i, c: u2r.at[i, :, :, c])
    q2 = Part("y", 2, lambda i, c: q2s.at[i, :, c], lambda i, c: q2r.at[i, :, c])
    d3 = Part("x", 3, lambda i, c: d3s.at[i, :, c], lambda i, c: d3r.at[i, :, c])

    def each(body):
        def step(c, carry):
            body(c)
            return carry
        lax.fori_loop(0, 3, step, 0)

    def shifted(lo, c):
        return pl.ds(pl.multiple_of(lo + c * STEP, STEP), STEP)

    def multiply(g, one):
        for c in fetched[g]:
            c.wait()
        arrived(1, g, 0)

        @pl.when(sec == 1)
        def _():
            partial[g].wait_recv()

        def across(c):
            spare = slice(SLOTS * R, (SLOTS + 1) * R)
            own = dr if g == W else wide[g]
            parts = [own[0:R, columns(c) if g == W else shifted(offsets[g][0], c)]]
            parts += [wide[g][spare, shifted(offsets[g][by], c)] for by in (1, 2, 3)]
            right = jnp.concatenate(parts, 0)
            for m in range(3):
                part = second[g].at[m * STEP:(m + 1) * STEP, columns(c)]
                held = jnp.where(sec == 1, part[...].astype(F32), 0.0)
                left = up_v[0:ROWS, g * D + m * STEP:g * D + (m + 1) * STEP]
                part[...] = (held + tn(left, right)).astype(BF16)
            one.start(c)
        each(across)

    def to_rows(dst):
        def store(i, at, value):
            dst[i, :, at] = value.astype(BF16)
        return store

    def twelve(rows):
        return jnp.concatenate([rows, jnp.zeros((4, STEP), F32)], 0).astype(BF16)

    def to_plane_u(y, at, value):
        for z in range(4):
            u4s[y, z, :, at] = twelve(value[12 * z:12 * z + 12])

    def to_plane_q(i, at, value):
        for x in range(4):
            for z in range(4):
                q4s[z, x, :, at] = twelve(value[48 * x + 12 * z:48 * x + 12 * z + 12])

    def to_out(i, at, value):
        d_out[:, at] = value

    def plane(g, src, dst):
        axis = "y" if g == U else "z"
        pos = rank(axis)
        return [pltpu.make_async_remote_copy(
            src_ref=src.at[lax.rem(pos + over, 4), peers[g][by]], dst_ref=dst.at[over, ranks[g]],
            send_sem=asend.at[g, over, by], recv_sem=arecv.at[g, over, ranks[g]],
            device_id={"dp": planes[g][over][by]}, device_id_type=MESH)
            for over in range(4) for by in range(4) if over or by]

    def plane_sum(g, dst, r):
        value = dst[0, r].astype(F32)
        for over in (1, 2, 3):
            value = value + dst[over, r].astype(F32)
        return value[0:12]

    def plane_arrived(g, dst):
        for over in range(4):
            for by in range(4):
                if over or by:
                    there = dst.at[over, peers[g][by]]
                    pltpu.make_async_remote_copy(
                        src_ref=there, dst_ref=there, send_sem=asend.at[g, 0, 0],
                        recv_sem=arecv.at[g, over, peers[g][by]],
                        device_id={"dp": places[g][1]}, device_id_type=MESH).wait_recv()

    multiply(W, d2)
    multiply(U, u2)
    multiply(Q, q2)
    share_next(0)

    for which in range(2):
        for g in range(3):
            for by in range(4):
                remote(which, g, 0, by).wait_send()

    @pl.when(sec == 1)
    def _():
        hand.wait_send()

        def drain(j, carry):
            for which in range(2):
                for g in range(3):
                    for by in range(4):
                        remote(which, g, j, by).wait_send()
            return carry
        lax.fori_loop(1, SLOTS, drain, 0)
    present.wait()

    def second_done(c):
        u2.finish(c, to_plane_u)
        d2.finish(c, to_rows(d3s))
        d3.start(c)
    each(second_done)
    spread_u = plane(U, u4s, u4r)
    for copy in spread_u:
        copy.start()
    u4r[0, ranks[U]] = u4s[rank("y"), ranks[U]]
    each(lambda c: q2.finish(c, to_plane_q))
    spread_q = plane(Q, q4s, q4r)
    for copy in spread_q:
        copy.start()
    q4r[0, ranks[Q]] = q4s[rank("z"), ranks[Q]]
    share_next(1)

    def drained(c):
        for one in (d2, u2, q2):
            one.drain(c)
    each(drained)
    each(lambda c: d3.finish(c, to_out))
    share_next(2)
    sums[...] = vec[3]
    other = partner_copy(vec.at[3], sums_other, vsem)
    other.start()
    plane_arrived(U, u4r)
    for i in range(4):
        u_out[:, i * D:(i + 1) * D] = plane_sum(U, u4r, i)
    plane_arrived(Q, q4r)
    for i in range(3):
        q_out[:, i * D:(i + 1) * D] = plane_sum(Q, q4r, i)
    o_out[...] = plane_sum(Q, q4r, 3)
    each(lambda c: d3.drain(c))
    for copies in shared + [spread_u, spread_q]:
        for copy in copies:
            copy.wait_send()
    other.wait()


def main(*args):
    vmem = pl.BlockSpec(memory_space=VM)
    hbm = pl.BlockSpec(memory_space=pltpu.HBM)
    dma = pltpu.SemaphoreType.DMA
    return pl.pallas_call(
        main_kernel,
        out_shape=[jax.ShapeDtypeStruct(dims, dtype) for dims, dtype in (
            ((2, 32, D), BF16), ((2, 32, D), BF16), ((12, 3 * D), F32), ((12, D), F32), ((12, FF), F32), ((48, D), F32),
            ((16, D), F32), ((16, D), F32), ((3, SLOTS + 1, 4, R, D), BF16), ((12, D, D), BF16))],
        in_specs=[vmem, vmem, pl.BlockSpec(memory_space=pltpu.SMEM), vmem] + [hbm] * 4 + [vmem] * 3,
        out_specs=[vmem] * 8 + [hbm] * 2,
        scratch_shapes=[
            VM((3, D, D), BF16), VM((D, D), BF16), VM((D, FF), BF16), VM((FF, D), BF16),
            VM((2, 256, D), BF16), VM((2, 256, D), BF16), VM((SLOTS, 6, 256, 256), F32),
            VM((SLOTS, R, D), F32), VM((SLOTS, R, 128), F32), VM((SLOTS, R, D), F32), VM((SLOTS, R, 128), F32),
            VM((SLOTS, R, FF), F32), VM((2, 256, D), F32), VM((2, 256, D), F32), VM((R, D), F32),
            VM((2, ROWS, D), BF16), VM((ROWS, D), BF16), VM((ROWS + R, FF), BF16), VM((ROWS + R, 4 * D), BF16),
            VM((ROWS + R, FF), BF16), VM((ROWS, D), BF16), VM((16, D), F32),
            VM((2, 2, 32, D), BF16), VM((R, D), BF16), VM((R, D), BF16), VM((2, 32, D), BF16),
            VM((SLOTS, 1, D), F32),
            VM((4, 192, D), BF16), VM((4, 4, 48, D), BF16), VM((4, 4, 48, D), BF16),
            VM((4, 48, D), BF16),
            VM((3, 192, D), BF16), VM((3, 4, 48, D), BF16), VM((3, 4, 48, D), BF16),
            VM((3, 48, D), BF16)]
        + [VM((4, 4, 16, D), BF16)] * 4 + [VM((4, 16, D), F32), VM((3, 3, 16, D), F32)]
        + [dma((6,)), dma((12,)), dma((10,)), dma((2,)), dma((2,)), dma((2,)), dma((3, 2)), dma((2,)),
           dma((2, 3, SLOTS, 4)), dma((2, 3, SLOTS, 4)), dma((3, 4)), dma((4, 3, 3)), dma((4, 3, 3)),
           dma((2, 4, 4)), dma((2, 4, 4)), dma((3, 3)), dma((3, 3))],
        compiler_params=pltpu.CompilerParams(collective_id=0, has_side_effects=True, vmem_limit_bytes=int(63.4 * 2**20)),
        name="layers",
    )(*args)


def finish_kernel(keep, got, q_in, o_in, u_in, d_in, sums, other,
                  hidden, token, q_out, o_out, u_out, d_out, g_gains, g_bias, g_up, g_embed):
    sec = lax.axis_index("section")
    dp = lax.axis_index("dp")
    hidden[...] = jnp.where(sec == 0, got[...], keep[...])
    token[...] = jnp.where(sec == 0, keep[...], got[...])
    for i in range(12):
        q_out[i] = q_in[i:i + 1, :]
        o_out[i] = o_in[i:i + 1, :]
        u_out[i] = u_in[i:i + 1, :]
    d_out[0] = d_in[...]
    turned = pltpu.roll(sums[...], lax.rem(D - dp * 12, D), 1)
    g_gains[0] = turned[0:2, 0:12]
    for i in range(6):
        g_bias[i] = turned[2 + i:3 + i, 0:12]
    lines = sums[12:13, :]
    for i in range(1, 4):
        lines = jnp.where(lax.div(dp, 16) == i, sums[12 + i:13 + i, :], lines)
    g_up[...] = pltpu.roll(lines, lax.rem(D - lax.rem(dp, 16) * 48, D), 1)[:, 0:48]
    mine, theirs = sums[8:12, :], other[8:12, :]
    rows = jnp.concatenate([jnp.where(sec == 0, mine, theirs)[0:1], jnp.where(sec == 0, theirs, mine)], 0)
    g_embed[...] = pltpu.roll(rows, lax.rem(D - (sec * 64 + dp) * 6, D), 1)[:, 0:6]


def finish(*args):
    vmem = pl.BlockSpec(memory_space=VM)
    return pl.pallas_call(
        finish_kernel,
        out_shape=[jax.ShapeDtypeStruct(dims, dtype) for dims, dtype in (
            ((2, 32, D), BF16), ((2, 32, D), BF16), ((12, 1, 3 * D), F32), ((12, 1, D), F32), ((12, 1, FF), F32),
            ((1, 48, D), F32), ((1, 2, 12), F32), ((6, 1, 12), F32), ((1, 48), F32), ((5, 6), F32))],
        in_specs=[vmem] * 8, out_specs=[vmem] * 10,
        name="finish",
    )(*args)


def local(*args):
    args = list(args)
    args[9] = jnp.swapaxes(args[9], 0, 1)
    outs = list(finish(*main(*args)[:8]))
    for i in (2, 3, 4, 7):
        outs[i] = jnp.swapaxes(outs[i], 0, 1)
    return tuple(outs)


def solution(mesh):
    split = ("section",)
    placed = (
        P("dp", "section", None), P("dp", "section", None), P("dp"), P(),
        P("section", None, None), P("section", None, None), P("section", None, None), P("section", None, None),
        P("section", None, None), P("section", None, None), P("section", None))
    return jax.shard_map(
        local, mesh=mesh, in_specs=placed,
        out_specs=(
            P("dp", "section", None), P("dp", "section", None),
            P("section", "dp", None), P("section", "dp", None), P("section", "dp", None), P("section", "dp", None),
            P("section", None, "dp"), P("section", None, "dp"), P("section", "dp"), P(None, ("section", "dp"))),
        check_vma=False)
```
